128 devices in a mesh: leaf: 4 (over x), col: 32 (over z, y, core).
Axes of the slice: x: 4, y: 4, z: 4, core: 2. Of those that a mesh axis runs over, the one named last changes fastest.
Arguments:
- incident: float32 [3072, 16384], P('leaf', 'col'), may hold values from -6 to 6
- sources: float32 [3072, 16384], P('leaf', 'col'), may hold values from -6 to 6
- tree_order: int32 [4, 768], P('leaf'), may hold values from 0 to 767, each once within a row
- near_quad: float32 [4096, 768], P('leaf'), may hold values from -0.21875 to 0.21875
- near_owner: int32 [4096, 1], P('leaf'), may hold values from 0 to 3; in each aligned block of 1024 rows (0 to 1023, 1024 to 2047, ...) at most 512 rows name the same one
- near_slot: int32 [4096], P('leaf'), may hold values from 0 to 767
- leaf_inverse: float32 [3072, 768], P(('leaf', 'col')), may hold values from -0.21875 to 0.21875
- basis_v: float32 [2, 3072, 128], P(None, ('leaf', 'col')), may hold values from -6 to 6
- basis_w: float32 [2, 2, 3072, 128], P(None, None, ('leaf', 'col')), may hold values from -0.125 to 0.125
Outputs:
- solution: float32 [3072, 16384], P('leaf', 'col')
The draws below stay inside these ranges and needn't reach their ends.
Inputs may be any that keep to these rules, and one draw needn't show every extreme that they name: `near_owner`: in the rows of one leaf block (aligned blocks of 1024 rows), no owner is named by more than 512 rows, a bound that some block reaches. Each row of tree_order names every number once.
All inputs are finite; a program needn't handle non-finite values.
Results may differ from the reference program's by a relative error of at most 0.0001.
Values sent between devices are 32-bit elements; how exact they have to be, the bound alone decides.
A program may use at most 192 MiB of HBM per device.

```python
import math
import jax
import jax.numpy as jnp
import numpy as np
from jax import lax

LEAF = 768
RANK = 128
NEAR_DEV = 1024
LEVELS = 2
CAP = 512
PANELS = 3072
NRHS = 16384
NEAR_TOTAL = 4096
N_LEAF = 4


def set_ends(array, own_key, smallest, top_value):
    place = [jax.random.randint(jax.random.fold_in(own_key, axis), (), 0, length) for axis, length in enumerate(array.shape)]
    widest = array.shape.index(max(array.shape))
    neighbour = place[:widest] + [(place[widest] + 1) % array.shape[widest]] + place[widest + 1:]
    return array.at[tuple(place)].set(smallest).at[tuple(neighbour)].set(top_value)


def steps_of(rng, shape, pieces, least, largest):
    level, own = 1.0, jax.random.fold_in(rng, 6)
    for axis_at, shards_of in pieces:
        draws = jnp.exp(jax.random.uniform(jax.random.fold_in(own, axis_at), (shards_of,), jnp.float32, least / len(pieces), largest / len(pieces)))
        level = level * jnp.repeat(draws, shape[axis_at] // shards_of).reshape([-1 if axis == axis_at else 1 for axis in range(len(shape))])
    return level


def deal_out(rng, own, number, rows, number_of, top, limit, lean):
    sequence = jax.random.permutation(rng, number_of)
    heavy_load, usual = portions_of(number_of, rows * top, limit, lean, True), portions_of(number_of, rows * top, limit, lean, False)
    places = jnp.arange(number_of)

    def named(lengths, rotation):
        used = int((lengths > 0).sum())
        fixed = max(1, used // 4)
        moved = fixed + (places - fixed + rotation * (used - fixed)) % max(1, number_of - fixed)
        return jnp.zeros((number_of,), jnp.int32).at[sequence[jnp.where(places < fixed, places, moved)]].set(jnp.asarray(lengths, jnp.int32))

    lengths = jnp.where(number % 4 == 0, named(heavy_load, number // 4), named(usual, number - number // 4 - 1))
    mixed = jax.random.permutation(jax.random.fold_in(own, 3), number_of)
    giver, sink = mixed[0:number_of // 2 * 2:2], mixed[1:number_of // 2 * 2:2]
    room = jnp.minimum(lengths[giver] - 1, limit - lengths[sink]) // 2
    room = jnp.where((giver == sequence[0]) | (sink == sequence[0]) | (lengths[sink] == 0), 0, jnp.maximum(room, 0))
    moved = jax.random.randint(jax.random.fold_in(own, 4), (number_of // 2,), 0, 1 << 20) % (room + 1)
    lengths = lengths.at[giver].add(-moved).at[sink].add(moved)
    labels = jnp.searchsorted(jnp.cumsum(lengths), jnp.arange(rows * top), side="right").astype(jnp.int32)
    listing = labels.reshape(top, rows).T
    listing = listing[jax.random.permutation(jax.random.fold_in(own, 1), rows)]
    rotation = jax.random.randint(jax.random.fold_in(own, 2), (rows, 1), 0, top)
    return jnp.take_along_axis(listing, (jnp.arange(top)[None, :] + rotation) % top, axis=1)


def portions_of(count, total, most, skew, full):
    portions = [(1 << 20) // math.isqrt(rank ** skew) + 1 for rank in range(1, count + 1)]
    largest = most if full else min(most, max(-(-total // count), total * portions[0] // sum(portions)))
    least = 1 if total - largest >= count - 1 else 0
    given, spare = [largest] + [least] * (count - 1), total - largest - least * (count - 1)
    while spare > 0:
        movable = [i for i in range(1, count) if given[i] < largest] or [i for i in range(1, count) if given[i] < most]
        whole, left = sum([portions[i] for i in movable]), spare
        for i in movable:
            addition = min(most - given[i], max(1, left * portions[i] // whole), spare)
            given[i] = given[i] + addition
            spare = spare - addition
    return np.array(given)


def scatter_about(key, dims, deviation, limit, split=(), held_as=jnp.bfloat16):
    drawn = deviation * jax.random.normal(key, dims, jnp.float32)
    if split:
        drawn = drawn * steps_of(key, dims, split, -0.22, 0.18)
    return jnp.clip(drawn, -limit, limit).astype(held_as)


def setup_inputs(seed: int = 0) -> dict:
    arg_keys = jax.random.split(jax.random.key(seed), 10)
    incident = scatter_about(arg_keys[0], (PANELS, NRHS), 1.0, 6.0, ((0, 4), (1, 32)), jnp.float32)
    sources = scatter_about(arg_keys[1], (PANELS, NRHS), 1.0, 6.0, ((0, 4), (1, 32)), jnp.float32)
    tree_order = jax.vmap(lambda own: jax.random.permutation(own, LEAF))(jax.random.split(arg_keys[2], N_LEAF)).reshape((N_LEAF, LEAF)).astype(jnp.int32)
    near_quad = scatter_about(arg_keys[3], (NEAR_TOTAL, LEAF), LEAF ** -0.5, 0.21875, ((0, 4),), jnp.float32)
    near_owner_keys = jax.random.split(jax.random.fold_in(arg_keys[4], 1), NEAR_TOTAL // NEAR_DEV)
    near_owner_turns = jax.random.permutation(jax.random.fold_in(arg_keys[4], 3), NEAR_TOTAL // NEAR_DEV)
    near_owner = jax.vmap(lambda own, number: deal_out(jax.random.fold_in(arg_keys[4], 2), own, number, NEAR_DEV, N_LEAF, 1, CAP, 2))(near_owner_keys, near_owner_turns).reshape((NEAR_TOTAL, 1))
    near_slot = set_ends(jax.random.randint(arg_keys[5], (NEAR_TOTAL,), 0, LEAF), jax.random.fold_in(arg_keys[5], 1), 0, LEAF - 1).astype(jnp.int32)
    leaf_inverse = scatter_about(arg_keys[6], (PANELS, LEAF), LEAF ** -0.5, 0.21875, ((0, 128),), jnp.float32)
    basis_v = scatter_about(arg_keys[7], (LEVELS, PANELS, RANK), 1.0, 6.0, ((1, 128),), jnp.float32)
    basis_w = scatter_about(arg_keys[8], (LEVELS, 2, PANELS, RANK), (20 * RANK) ** -0.5, 0.125, ((2, 128),), jnp.float32)
    return {"incident": incident, "sources": sources, "tree_order": tree_order, "near_quad": near_quad, "near_owner": near_owner, "near_slot": near_slot, "leaf_inverse": leaf_inverse, "basis_v": basis_v, "basis_w": basis_w}


def reference(incident, sources, tree_order, near_quad, near_owner, near_slot, leaf_inverse, basis_v, basis_w):
    high = lax.Precision.HIGHEST
    quad = near_quad.reshape(N_LEAF, NEAR_DEV, LEAF)
    strengths = sources.reshape(N_LEAF, LEAF, NRHS)
    partial_value = jnp.einsum('kqp,kpn->kqn', quad, strengths, precision=high).reshape(NEAR_TOTAL, NRHS)
    target = (near_owner[:, 0] * LEAF + near_slot).astype(jnp.int32)
    assembled = incident.at[target].add(partial_value)
    position = (jnp.arange(N_LEAF, dtype=jnp.int32)[:, None] * LEAF + tree_order).reshape(-1).astype(jnp.int32)
    ordered = assembled[position]
    inverse = leaf_inverse.reshape(N_LEAF, LEAF, LEAF)
    state = jnp.einsum('kab,kbn->kan', inverse, ordered.reshape(N_LEAF, LEAF, NRHS), precision=high).reshape(PANELS, NRHS)
    for level in range(1, LEVELS + 1):
        group = 2 ** (level - 1)
        child_count = N_LEAF // group
        rows = group * LEAF
        scale = 1.0 / math.sqrt(rows)
        shaped = state.reshape(child_count, rows, NRHS)
        vbasis = basis_v[level - 1].reshape(child_count, rows, RANK)
        coeff = jnp.einsum('cpr,cpn->crn', vbasis, shaped, precision=high) * scale
        sibling = coeff.reshape(child_count // 2, 2, RANK, NRHS)[:, ::-1].reshape(child_count, RANK, NRHS)
        wfirst = basis_w[level - 1, 0].reshape(child_count, rows, RANK)
        wsecond = basis_w[level - 1, 1].reshape(child_count, rows, RANK)
        update = jnp.einsum('cpr,crn->cpn', wfirst, sibling, precision=high) + jnp.einsum('cpr,crn->cpn', wsecond, coeff, precision=high)
        state = state - update.reshape(PANELS, NRHS)
    solution = jnp.zeros((PANELS, NRHS), jnp.float32).at[position].set(state)
    return solution
```

```python
import functools
import math

import jax
import jax.numpy as jnp
from jax import lax
from jax.experimental import pallas as pl
from jax.experimental.pallas import tpu as pltpu
from jax.sharding import PartitionSpec as P

MESH = pl.DeviceIdType.MESH
F32 = jnp.float32
BF16 = jnp.bfloat16
LANES = 128
RING = 4


def halves(value):
    top = value.astype(BF16)
    return top, (value - top.astype(F32)).astype(BF16)


def dot(a, b):
    return jnp.dot(a, b, preferred_element_type=F32)


def dot3(a_hi, a_lo, b_hi, b_lo):
    return dot(a_hi, b_hi) + dot(a_hi, b_lo) + dot(a_lo, b_hi)


def tiles(count, size, body):
    def step(index, carry):
        body(pl.ds(pl.multiple_of(index * size, size), size))
        return carry

    lax.fori_loop(0, count // size, step, 0)


class Place:
    def __init__(self):
        self.leaf = lax.axis_index("leaf")
        self.col = lax.axis_index("col")
        self.core = self.col % 2
        y = (self.col // 2) % RING
        z = self.col // (2 * RING)
        self.d1 = y * (1 - self.core) + z * self.core
        self.d2 = z * (1 - self.core) + y * self.core
        self.twin = (self.leaf, self.col + 1 - 2 * self.core)
        self.mate = (self.leaf + 1 - 2 * (self.leaf % 2), self.col)
        self.cross = (3 - self.leaf, self.col)
        self.right1 = (self.leaf, self.index(self.core, 0, 1))
        self.left1 = (self.leaf, self.index(self.core, 0, RING - 1))
        self.right2 = (self.leaf, self.index(self.core, 1, 0))
        self.left2 = (self.leaf, self.index(self.core, RING - 1, 0))

    def index(self, core, off2, off1):
        a, b = (self.d2 + off2) % RING, (self.d1 + off1) % RING
        return (a * 2 * RING + b * 2) * (1 - core) + (b * 2 * RING + a * 2 + 1) * core

    def twin_index(self, off2, off1):
        core = 1 - self.core
        a, b = (self.d1 + off2) % RING, (self.d2 + off1) % RING
        return (a * 2 * RING + b * 2) * (1 - core) + (b * 2 * RING + a * 2 + 1) * core


class Gather:
    def __init__(self, place, buf, send_sem, recv_sem):
        self.p, self.buf, self.ss, self.rs = place, buf, send_sem, recv_sem
        self.half = buf.shape[2] // 2
        self.started = []

    def piece(self, off2, off1, part=None):
        ref = self.buf.at[self.p.index(self.p.core, off2, off1)]
        return ref if part is None else ref.at[:, pl.ds(part * self.half, self.half)]

    def send(self, ref, sem, device):
        copy = pltpu.make_async_remote_copy(
            src_ref=ref, dst_ref=ref, send_sem=self.ss.at[sem], recv_sem=self.rs.at[sem],
            device_id=device, device_id_type=MESH,
        )
        copy.start()
        self.started.append(copy)

    def recv(self, ref, sem):
        pltpu.make_async_remote_copy(
            src_ref=ref, dst_ref=ref, send_sem=self.ss.at[sem], recv_sem=self.rs.at[sem],
            device_id=self.p.twin, device_id_type=MESH,
        ).wait_recv()

    def ring1(self):
        self.send(self.piece(0, 0), 0, self.p.right1)
        self.send(self.piece(0, 0), 1, self.p.left1)

    def ring1_pass(self):
        self.recv(self.piece(0, 3), 0)
        self.send(self.piece(0, 3, 0), 2, self.p.right1)
        self.recv(self.piece(0, 1), 1)
        self.send(self.piece(0, 1, 1), 3, self.p.left1)

    def ring1_end(self):
        self.recv(self.piece(0, 2, 0), 2)
        self.recv(self.piece(0, 2, 1), 3)

    def ring2(self, off1):
        self.send(self.piece(0, off1), 4 + off1, self.p.right2)
        self.send(self.piece(0, off1), 8 + off1, self.p.left2)

    def ring2_pass(self, off1):
        self.recv(self.piece(3, off1), 4 + off1)
        if off1 in (0, 3):
            self.send(self.piece(3, off1), 12 + off1, self.p.right2)
        self.recv(self.piece(1, off1), 8 + off1)
        if off1 in (1, 2):
            self.send(self.piece(1, off1), 12 + off1, self.p.left2)

    def ring2_end(self, off1):
        self.recv(self.piece(2, off1), 12 + off1)

    def to_twin(self, off2, off1):
        self.send(self.piece(off2, off1), 16 + 4 * off2 + off1, self.p.twin)

    def from_twin(self):
        for off2 in range(RING):
            for off1 in range(RING):
                ref = self.buf.at[self.p.twin_index(off2, off1)]
                self.recv(ref, 16 + 4 * off2 + off1)

    def finish(self):
        for copy in self.started:
            copy.wait_send()


def kernel(
    tree, owner, slot, inverse, basis_v, basis_w, incident, sources, near_quad, out,
    nq, s_own, x, nqp, wt, key_out, key_in, s_in, y_out, y_in, z_out, z_in, t_out, t_in, m_out, m_in, acc,
    nq_hi, nq_lo, s_hi, s_lo, p_hi, p_lo, oh, gt, vt_hi, vt_lo, b_hi, b_lo, ws_hi, ws_lo, wall_hi, wall_lo,
    k_hi, k_lo, x_hi, x_lo, c_hi, c_lo,
    gsend, grecv, csend, crecv, osend, orecv, load_sem, out_sem,
):
    leaf, cols = incident.shape
    near = near_quad.shape[0]
    rank = basis_v.shape[2]
    part = near // nqp.shape[0]
    chunks = cols // LANES
    big = min(256, leaf)
    wide = min(256, cols)
    place = Place()
    mine = place.col
    started = []

    def send(src, dst, sems, index, device):
        copy = pltpu.make_async_remote_copy(
            src_ref=src, dst_ref=dst, send_sem=sems[0].at[index], recv_sem=sems[1].at[index],
            device_id=device, device_id_type=MESH,
        )
        copy.start()
        started.append(copy)
        return copy

    def left(copy):
        copy.wait_send()
        started[:] = [other for other in started if other is not copy]

    def lane(i):
        return pl.ds(i * LANES, LANES)

    loads = [
        pltpu.make_async_copy(src, dst, load_sem.at[i])
        for i, (src, dst) in enumerate(((near_quad, nq), (sources, s_own), (incident, x)))
    ]
    for copy in loads:
        copy.start()
    key_out[...] = jnp.broadcast_to(owner[...] * leaf + slot[...], key_out.shape)

    barrier = pltpu.get_barrier_semaphore()
    neighbours = (
        place.mate, place.cross, place.twin, place.right1, place.left1, place.right2, place.left2
    )
    for device in neighbours:
        pl.semaphore_signal(barrier, inc=1, device_id=device, device_id_type=MESH)
    pl.semaphore_wait(barrier, len(neighbours))

    once, per = (osend, orecv), (csend, crecv)
    rows_mine = pl.ds(pl.multiple_of(mine * part, part), part)
    near_swap = send(near_quad.at[rows_mine], nqp.at[mine], once, 0, place.mate)
    key_swap = send(key_out, key_in, once, 1, place.mate)
    source_swaps = []

    def swap_sources(i):
        source_swaps.append(send(sources.at[:, lane(i)], s_in.at[i], per, (0, i), place.mate))

    for i in range(min(2, chunks)):
        swap_sources(i)

    near_g = Gather(place, nqp, gsend.at[0], grecv.at[0])
    wt_g = Gather(place, wt, gsend.at[1], grecv.at[1])

    def make_gt(rows):
        number = rows.start + lax.broadcasted_iota(jnp.int32, (rows.size, leaf), 0)
        gt[rows, :] = jnp.where(number == tree[...], 1.0, 0.0).astype(BF16)

    tiles(leaf, LANES, make_gt)
    nt = (((1,), (1,)), ((), ()))
    top, low = halves(inverse[...])
    wt[mine, :, pl.ds(0, leaf)] = lax.dot_general(
        top, gt[...], nt, preferred_element_type=F32
    ) + lax.dot_general(low, gt[...], nt, preferred_element_type=F32)
    for k in range(4):
        wt[mine, :, pl.ds(leaf + k * rank, rank)] = basis_w[k // 2, k % 2]
    for k in range(2):
        wt[mine, :, pl.ds(leaf + (4 + k) * rank, rank)] = basis_v[k]
    wt_g.ring1()
    wt_g.ring2(0)

    def make_one_hot(which, key, device):
        base = device[0] * leaf

        def body(rows):
            number = base + rows.start + lax.broadcasted_iota(jnp.int32, (rows.size, near), 0)
            oh[which, rows, :] = jnp.where(number == key[0:1, :], 1.0, 0.0).astype(BF16)

        tiles(leaf, LANES, body)

    me = (place.leaf, place.col)
    make_one_hot(0, key_out, me)
    make_one_hot(1, key_out, place.cross)
    loads[0].wait()

    def split_own(rows):
        nq_hi[rows, :], nq_lo[rows, :] = halves(nq[rows, :])

    tiles(near, LANES, split_own)

    near_swap.wait_recv()
    near_g.ring1()
    near_g.ring2(0)
    near_g.to_twin(0, 0)

    loads[1].wait()

    def split_sources(rows):
        s_hi[rows, :], s_lo[rows, :] = halves(s_own[rows, :])

    tiles(leaf, LANES, split_sources)

    def own_partial(block):
        def body(rows):
            r = dot3(nq_hi[rows, :], nq_lo[rows, :], s_hi[:, block], s_lo[:, block])
            p_hi[rows, block], p_lo[rows, block] = halves(r)

        tiles(near, big, body)

    blocks = [pl.ds(k * wide, wide) for k in range(cols // wide)]
    for block in blocks[: len(blocks) // 2]:
        own_partial(block)
    near_g.ring1_pass()
    for off1 in (3, 1):
        near_g.ring2(off1)
        near_g.to_twin(0, off1)
    for block in blocks[len(blocks) // 2 :]:
        own_partial(block)
    near_g.ring1_end()
    near_g.ring2(2)
    near_g.to_twin(0, 2)
    wt_g.ring1_pass()

    loads[2].wait()

    def own_sums(block):
        def body(rows):
            x[rows, block] += dot(oh[0, rows, :], p_hi[:, block]) + dot(oh[0, rows, :], p_lo[:, block])
            r = dot(oh[1, rows, :], p_hi[:, block]) + dot(oh[1, rows, :], p_lo[:, block])
            for k in range(wide // LANES):
                y_out[block.start // LANES + k, rows, :] = r[:, k * LANES : (k + 1) * LANES]

        tiles(leaf, big, body)

    for block in blocks[: len(blocks) // 2]:
        own_sums(block)
    wt_g.ring1_end()
    wt_g.to_twin(0, 0)
    wt_g.to_twin(0, 1)
    wt_g.to_twin(0, 2)
    wt_g.to_twin(0, 3)
    for off1 in (0, 3, 1):
        near_g.ring2_pass(off1)
        near_g.to_twin(3, off1)
        near_g.to_twin(1, off1)
    for block in blocks[len(blocks) // 2 :]:
        own_sums(block)
    near_g.ring2_pass(2)
    near_g.to_twin(3, 2)
    near_g.to_twin(1, 2)
    for off1 in (3, 1, 2):
        wt_g.ring2(off1)
    if chunks > 2:
        left(source_swaps[0])
        swap_sources(2)
    key_swap.wait_recv()
    make_one_hot(2, key_in, me)
    make_one_hot(3, key_in, place.cross)
    for off1 in (0, 3, 1, 2):
        near_g.ring2_end(off1)
        near_g.to_twin(2, off1)
    near_g.from_twin()

    def split_partner(index, carry):
        rows = pl.ds(pl.multiple_of(index * part, part), part)
        nq_hi[rows, :], nq_lo[rows, :] = halves(nqp[index])
        return carry

    lax.fori_loop(0, nqp.shape[0], split_partner, 0)

    sum_swaps, z_swaps, t_swaps, stores = {}, {}, {}, {}

    def near_chunk(i):
        source_swaps[i].wait_recv()

        def split(rows):
            s_hi[rows, lane(i)], s_lo[rows, lane(i)] = halves(s_in[i, rows, :])

        tiles(leaf, LANES, split)

        def partial(rows):
            r = dot3(nq_hi[rows, :], nq_lo[rows, :], s_hi[:, lane(i)], s_lo[:, lane(i)])
            p_hi[rows, lane(i)], p_lo[rows, lane(i)] = halves(r)

        tiles(near, big, partial)

        def across(rows):
            y_out[i, rows, :] += dot(oh[3, rows, :], p_hi[:, lane(i)]) + dot(
                oh[3, rows, :], p_lo[:, lane(i)]
            )

        tiles(leaf, big, across)
        sum_swaps[i] = send(y_out.at[i], y_in.at[i], per, (1, i), place.cross)

        def here(rows):
            x[rows, lane(i)] += dot(oh[2, rows, :], p_hi[:, lane(i)]) + dot(
                oh[2, rows, :], p_lo[:, lane(i)]
            )

        tiles(leaf, big, here)

    def weights():
        def split(index, carry):
            count = 2 * inverse.shape[0]
            rows = pl.ds(pl.multiple_of(index * count, 16), count)
            both = wt[pl.ds(2 * index, 2), :, pl.ds(0, leaf + 4 * rank)]
            ws_hi[rows, :], ws_lo[rows, :] = halves(both.reshape(count, leaf + 4 * rank))
            return carry

        lax.fori_loop(0, wt.shape[0] // 2, split, 0)
        for k in range(2):
            v = wt[:, :, pl.ds(leaf + (4 + k) * rank, rank)].reshape(leaf, rank)
            v = v * (1.0 / math.sqrt(2**k * leaf))
            rows = pl.ds(k * rank, rank)
            vt_hi[rows, :], vt_lo[rows, :] = halves(v.T)
        last = pl.ds(rank, rank)
        first_w = pl.ds(leaf, 2 * rank)
        m_out[...] = dot3(vt_hi[last, :], vt_lo[last, :], ws_hi[:, first_w], ws_lo[:, first_w])
        swap = send(m_out, m_in, once, 2, place.mate)
        step = min(256, leaf)
        for k in range(leaf // step):
            block = pl.ds(k * step, step)

            def body(rows):
                r = dot3(vt_hi[rows, :], vt_lo[rows, :], ws_hi[:, block], ws_lo[:, block])
                b_hi[rows, block], b_lo[rows, block] = halves(r)

            tiles(2 * rank, rank, body)
        for k in range((leaf + 4 * rank) // step):
            block = pl.ds(k * step, step)
            sign = 1.0 if k * step < leaf else -1.0

            def body(rows):
                wall_hi[rows, block] = (dot(gt[rows, :], ws_hi[:, block]) * sign).astype(BF16)
                wall_lo[rows, block] = (dot(gt[rows, :], ws_lo[:, block]) * sign).astype(BF16)

            tiles(leaf, big, body)
        swap.wait_recv()
        one, two = pl.ds(0, rank), pl.ds(rank, rank)
        k_hi[:, one], k_lo[:, one] = halves(m_out[:, one] + m_in[:, two])
        k_hi[:, two], k_lo[:, two] = halves(m_out[:, two] + m_in[:, one])

    def apply(rows, at, size, v_hi, v_lo):
        block = pl.ds(at, size)
        return dot3(wall_hi[rows, block], wall_lo[rows, block], v_hi, v_lo)

    def first(i):
        sum_swaps[i].wait_recv()

        def split(rows):
            x_hi[rows, :], x_lo[rows, :] = halves(x[rows, lane(i)] + y_in[i, rows, :])

        tiles(leaf, LANES, split)

        def coefficients(rows):
            z_out[i, rows, :] = dot3(b_hi[rows, :], b_lo[rows, :], x_hi[...], x_lo[...])

        tiles(2 * rank, rank, coefficients)
        z_swaps[i] = send(z_out.at[i], z_in.at[i], per, (2, i), place.mate)

        def state(rows):
            acc[rows, lane(i)] = apply(rows, 0, leaf, x_hi[...], x_lo[...])

        tiles(leaf, big, state)

    def second(i):
        z_swaps[i].wait_recv()
        one, two = pl.ds(0, rank), pl.ds(rank, rank)
        c_hi[one, :], c_lo[one, :] = halves(z_in[i, one, :])
        c_hi[two, :], c_lo[two, :] = halves(z_out[i, one, :])
        change = dot3(k_hi[...], k_lo[...], c_hi[...], c_lo[...])
        total = z_out[i, two, :] + z_in[i, two, :] - change
        t_out[i] = total
        t_swaps[i] = send(t_out.at[i], t_in.at[i], per, (3, i), place.cross)
        t_hi, t_lo = halves(total)

        def update(rows):
            acc[rows, lane(i)] += apply(rows, leaf, 2 * rank, c_hi[...], c_lo[...]) + apply(
                rows, leaf + 3 * rank, rank, t_hi, t_lo
            )

        tiles(leaf, big, update)

    def third(i):
        t_swaps[i].wait_recv()
        t_hi, t_lo = halves(t_in[i])

        def update(rows):
            acc[rows, lane(i)] += apply(rows, leaf + 2 * rank, rank, t_hi, t_lo)

        tiles(leaf, big, update)
        stores[i] = pltpu.make_async_copy(acc.at[:, lane(i)], out.at[:, lane(i)], out_sem.at[i])
        stores[i].start()

    near_chunk(0)
    for off1 in (0, 3, 1, 2):
        wt_g.ring2_pass(off1)
        wt_g.to_twin(3, off1)
        wt_g.to_twin(1, off1)
    if chunks > 3:
        left(source_swaps[1])
        swap_sources(3)
    near_chunk(1)
    for off1 in (0, 3, 1, 2):
        wt_g.ring2_end(off1)
        wt_g.to_twin(2, off1)
    for i in range(2, chunks - 1):
        near_chunk(i)
    wt_g.from_twin()
    weights()
    first(0)
    if chunks > 2:
        near_chunk(chunks - 1)
    for i in range(1, chunks):
        first(i)
        second(i - 1)
        if i > 1:
            third(i - 2)
    second(chunks - 1)
    if chunks > 1:
        third(chunks - 2)
    third(chunks - 1)

    for i in range(chunks):
        stores[i].wait()
    for copy in started:
        copy.wait_send()
    near_g.finish()
    wt_g.finish()


def per_device(
    incident, sources, tree_order, near_quad, near_owner, near_slot, leaf_inverse, basis_v, basis_w
):
    leaf, cols = incident.shape
    near = near_quad.shape[0]
    rank = basis_v.shape[2]
    group = lax.axis_size("col")
    rows = leaf // group
    chunks = cols // LANES
    width = leaf + 6 * rank
    vmem, sem = pltpu.VMEM, pltpu.SemaphoreType.DMA

    def f32(*shape):
        return vmem(shape, F32)

    def pair(*shape):
        return [vmem(shape, BF16), vmem(shape, BF16)]

    scratch = [
        f32(near, leaf), f32(leaf, cols), f32(leaf, cols),
        f32(group, near // group, leaf), f32(group, rows, width),
        vmem((8, near), jnp.int32), vmem((8, near), jnp.int32),
        f32(chunks, leaf, LANES), f32(chunks, leaf, LANES), f32(chunks, leaf, LANES),
        f32(chunks, 2 * rank, LANES), f32(chunks, 2 * rank, LANES),
        f32(chunks, rank, LANES), f32(chunks, rank, LANES),
        f32(rank, 2 * rank), f32(rank, 2 * rank), f32(leaf, cols),
        *pair(near, leaf), *pair(leaf, cols), *pair(near, cols),
        vmem((4, leaf, near), BF16), vmem((leaf, leaf), BF16),
        *pair(2 * rank, leaf), *pair(2 * rank, leaf),
        *pair(leaf, leaf + 4 * rank), *pair(leaf, leaf + 4 * rank),
        *pair(rank, 2 * rank), *pair(leaf, LANES), *pair(2 * rank, LANES),
        sem((2, 32)), sem((2, 32)), sem((4, chunks)), sem((4, chunks)), sem((3,)), sem((3,)),
        sem((3,)), sem((chunks,)),
    ]
    in_vmem = pl.BlockSpec(memory_space=pltpu.VMEM)
    in_any = pl.BlockSpec(memory_space=pl.ANY)
    return pl.pallas_call(
        kernel,
        out_shape=jax.ShapeDtypeStruct((leaf, cols), F32),
        in_specs=[in_vmem] * 6 + [in_any] * 3,
        out_specs=in_any,
        scratch_shapes=scratch,
        compiler_params=pltpu.CompilerParams(
            collective_id=0, has_side_effects=True, vmem_limit_bytes=60 * 1024 * 1024
        ),
        cost_estimate=pl.CostEstimate(flops=15 * 10**9, bytes_accessed=12 * 10**6, transcendentals=0),
    )(
        tree_order, near_owner.reshape(1, near), near_slot.reshape(1, near),
        leaf_inverse, basis_v, basis_w, incident, sources, near_quad,
    )


def solution(mesh):
    placed = (
        P("leaf", "col"),
        P("leaf", "col"),
        P("leaf", None),
        P("leaf", None),
        P("leaf", None),
        P("leaf"),
        P(("leaf", "col"), None),
        P(None, ("leaf", "col"), None),
        P(None, None, ("leaf", "col"), None),
    )
    return jax.shard_map(
        per_device, mesh=mesh, in_specs=placed, out_specs=P("leaf", "col"), check_vma=False
    )
```

```python
import functools
import math

import jax
import jax.numpy as jnp
from jax import lax
from jax.experimental import pallas as pl
from jax.experimental.pallas import tpu as pltpu
from jax.sharding import PartitionSpec as P

MESH = pl.DeviceIdType.MESH
F32 = jnp.float32
BF16 = jnp.bfloat16
LANES = 128
RING = 4


def halves(value):
    top = value.astype(BF16)
    return top, (value - top.astype(F32)).astype(BF16)


def dot(a, b):
    return jnp.dot(a, b, preferred_element_type=F32)


def dot3(a_hi, a_lo, b_hi, b_lo):
    return dot(a_hi, b_hi) + dot(a_hi, b_lo) + dot(a_lo, b_hi)


def beside(value):
    return jnp.concatenate(halves(value), axis=1)


def fold(wide):
    return wide[:, :LANES] + wide[:, LANES:]


def dot_beside(a_hi, a_lo, b):
    return fold(dot(a_hi, b)) + dot(a_lo, b[:, :LANES])


def tiles(count, size, body):
    def step(index, carry):
        body(pl.ds(pl.multiple_of(index * size, size), size))
        return carry

    lax.fori_loop(0, count // size, step, 0)


class Place:
    def __init__(self):
        self.leaf = lax.axis_index("leaf")
        self.col = lax.axis_index("col")
        self.core = self.col % 2
        y = (self.col // 2) % RING
        z = self.col // (2 * RING)
        self.d1 = y * (1 - self.core) + z * self.core
        self.d2 = z * (1 - self.core) + y * self.core
        self.twin = (self.leaf, self.col + 1 - 2 * self.core)
        self.mate = (self.leaf + 1 - 2 * (self.leaf % 2), self.col)
        self.cross = (3 - self.leaf, self.col)
        self.right1 = (self.leaf, self.index(self.core, 0, 1))
        self.left1 = (self.leaf, self.index(self.core, 0, RING - 1))
        self.opposite1 = (self.leaf, self.index(self.core, 0, 2))
        self.far = self.leaf + 2 - 4 * (self.leaf // 2)
        self.right2 = (self.leaf, self.index(self.core, 1, 0))
        self.left2 = (self.leaf, self.index(self.core, RING - 1, 0))

    def index(self, core, off2, off1):
        a, b = (self.d2 + off2) % RING, (self.d1 + off1) % RING
        return (a * 2 * RING + b * 2) * (1 - core) + (b * 2 * RING + a * 2 + 1) * core

    def twin_index(self, off2, off1):
        core = 1 - self.core
        a, b = (self.d1 + off2) % RING, (self.d2 + off1) % RING
        return (a * 2 * RING + b * 2) * (1 - core) + (b * 2 * RING + a * 2 + 1) * core


class Gather:
    def __init__(self, place, buf, send_sem, recv_sem):
        self.p, self.buf, self.ss, self.rs = place, buf, send_sem, recv_sem
        self.started = []

    def piece(self, off2, off1):
        return self.buf.at[self.p.index(self.p.core, off2, off1)]

    def send(self, ref, sem, device):
        copy = pltpu.make_async_remote_copy(
            src_ref=ref, dst_ref=ref, send_sem=self.ss.at[sem], recv_sem=self.rs.at[sem],
            device_id=device, device_id_type=MESH,
        )
        copy.start()
        self.started.append(copy)

    def recv(self, ref, sem):
        pltpu.make_async_remote_copy(
            src_ref=ref, dst_ref=ref, send_sem=self.ss.at[sem], recv_sem=self.rs.at[sem],
            device_id=self.p.twin, device_id_type=MESH,
        ).wait_recv()

    def ring1(self):
        own = self.piece(0, 0)
        self.send(own, 0, self.p.right1)
        self.send(own, 1, self.p.left1)
        self.send(own, 2, self.p.opposite1)

    def ring1_end(self):
        for sem, off1 in enumerate((3, 1, 2)):
            self.recv(self.piece(0, off1), sem)

    def ring2(self, off1):
        self.send(self.piece(0, off1), 4 + off1, self.p.right2)
        self.send(self.piece(0, off1), 8 + off1, self.p.left2)

    def ring2_pass(self, off1):
        self.recv(self.piece(3, off1), 4 + off1)
        if off1 in (0, 3):
            self.send(self.piece(3, off1), 12 + off1, self.p.right2)
        self.recv(self.piece(1, off1), 8 + off1)
        if off1 in (1, 2):
            self.send(self.piece(1, off1), 12 + off1, self.p.left2)

    def ring2_end(self, off1):
        self.recv(self.piece(2, off1), 12 + off1)

    def to_twin(self, off2, off1):
        self.send(self.piece(off2, off1), 16 + 4 * off2 + off1, self.p.twin)

    def from_twin(self):
        for off2 in range(RING):
            for off1 in range(RING):
                ref = self.buf.at[self.p.twin_index(off2, off1)]
                self.recv(ref, 16 + 4 * off2 + off1)

    def finish(self):
        for copy in self.started:
            copy.wait_send()


def kernel(
    tree_any, owner_any, slot_any, inverse_any, basis_v_any, basis_w_any, incident, sources, near_quad, out,
    tree, owner, slot, inverse, basis_v, basis_w,
    nq, s_own, x, nqp, wt, key_out, key_in, s_in, y_out, y_in, z_out, z_in, t_out, t_in, u_out, u_in, w_out, w_in,
    m_out, m_in, acc,
    nq_hi, nq_lo, s_hl, p_hl, oh, gt, vt_hi, vt_lo, b_hi, b_lo, ws_hi, ws_lo, wall_hi, wall_lo,
    k_hi, k_lo, x_hl, c_hl,
    gsend, grecv, csend, crecv, osend, orecv, load_sem, out_sem,
):
    leaf, cols = incident.shape
    near = near_quad.shape[0]
    rank = basis_v.shape[2]
    part = near // nqp.shape[0]
    chunks = cols // LANES
    last = chunks - 1
    near_tile, leaf_tile = near // 2, leaf // 2
    place = Place()
    mine = place.col
    started = []

    def lane(i):
        return pl.ds(i * LANES, LANES)

    pairs = (
        (tree_any, tree), (owner_any, owner), (slot_any, slot), (inverse_any, inverse), (basis_v_any, basis_v),
        (basis_w_any, basis_w), (near_quad, nq), (sources, s_own), (incident, x),
    )
    loads = [pltpu.make_async_copy(src, dst, load_sem.at[i]) for i, (src, dst) in enumerate(pairs)]
    barrier = pltpu.get_barrier_semaphore()
    neighbours = (
        place.mate, place.cross, place.twin, place.right1, place.left1, place.opposite1, place.right2, place.left2
    )
    for device in neighbours:
        pl.semaphore_signal(barrier, inc=1, device_id=device, device_id_type=MESH)
    for copy in loads:
        copy.start()

    def send(src, dst, sems, index, device):
        copy = pltpu.make_async_remote_copy(
            src_ref=src, dst_ref=dst, send_sem=sems[0].at[index], recv_sem=sems[1].at[index],
            device_id=device, device_id_type=MESH,
        )
        copy.start()
        started.append(copy)
        return copy

    near_g = Gather(place, nqp, gsend.at[0], grecv.at[0])
    wt_g = Gather(place, wt, gsend.at[1], grecv.at[1])

    def make_gt(rows):
        number = rows.start + lax.broadcasted_iota(jnp.int32, (rows.size, leaf), 0)
        gt[rows, :] = jnp.where(number == tree[...], 1.0, 0.0).astype(BF16)

    def make_one_hot(which, key, block):
        base = block * leaf

        def body(rows):
            number = base + rows.start + lax.broadcasted_iota(jnp.int32, (rows.size, near), 0)
            oh[which, rows, :] = jnp.where(number == key[0:1, :], 1.0, 0.0).astype(BF16)

        tiles(leaf, LANES, body)

    def split_near(rows):
        nq_hi[rows, :], nq_lo[rows, :] = halves(nq[rows, :])

    def partial(i):
        def body(rows):
            p_hl[i, rows, :] = beside(dot_beside(nq_hi[rows, :], nq_lo[rows, :], s_hl[i]))

        tiles(near, near_tile, body)

    def own_partial(i):
        def body(rows):
            s_hl[i, rows, :] = beside(s_own[rows, lane(i)])

        tiles(leaf, LANES, body)
        partial(i)

    def sums(which, i, rows):
        return fold(dot(oh[which, rows, :], p_hl[i]))

    for copy in loads[:6]:
        copy.wait()
    key_out[...] = jnp.broadcast_to(owner[...] * leaf + slot[...], key_out.shape)
    tiles(leaf, LANES, make_gt)
    nt = (((1,), (1,)), ((), ()))
    top, low = halves(inverse[...])
    wt[mine, :, pl.ds(0, leaf)] = lax.dot_general(
        top, gt[...], nt, preferred_element_type=F32
    ) + lax.dot_general(low, gt[...], nt, preferred_element_type=F32)
    for k in range(4):
        wt[mine, :, pl.ds(leaf + k * rank, rank)] = basis_w[k // 2, k % 2]
    for k in range(2):
        wt[mine, :, pl.ds(leaf + (4 + k) * rank, rank)] = basis_v[k]
    make_one_hot(1, key_out, place.cross[0])
    make_one_hot(3, key_out, place.far)
    loads[6].wait()
    tiles(near, LANES, split_near)
    loads[7].wait()
    own_partial(last)

    pl.semaphore_wait(barrier, len(neighbours))

    once, per = (osend, orecv), (csend, crecv)
    rows_mine = pl.ds(pl.multiple_of(mine * part, part), part)
    near_swap = send(near_quad.at[rows_mine], nqp.at[mine], once, 0, place.mate)
    key_swap = send(key_out, key_in, once, 1, place.mate)
    wt_g.ring1()
    wt_g.ring2(0)
    wt_g.to_twin(0, 0)
    source_swaps = [
        send(sources.at[:, lane(i)], s_in.at[i], per, (0, i), place.mate) for i in range(last)
    ]

    def last_across(rows):
        y_out[last, rows, :] = sums(1, last, rows)

    tiles(leaf, leaf_tile, last_across)
    sum_swaps = {last: send(y_out.at[last], y_in.at[last], per, (1, last), place.cross)}

    def last_far(rows):
        w_out[rows, :] = sums(3, last, rows)

    tiles(leaf, leaf_tile, last_far)
    far_swap = send(w_out, w_in, once, 3, place.cross)
    make_one_hot(2, key_out, place.mate[0])
    make_one_hot(0, key_out, place.leaf)

    near_swap.wait_recv()
    near_g.ring1()
    near_g.ring2(0)
    near_g.to_twin(0, 0)

    for i in range(last):
        own_partial(i)
    near_g.ring1_end()
    for off1 in (3, 1, 2):
        near_g.ring2(off1)
    for off1 in (3, 1, 2):
        near_g.to_twin(0, off1)
    wt_g.ring1_end()
    for off1 in (3, 1, 2):
        wt_g.to_twin(0, off1)
    loads[8].wait()

    def own_sums(i):
        def body(rows):
            x[rows, lane(i)] += sums(0, i, rows)
            if i < last:
                y_out[i, rows, :] = sums(1, i, rows)
            else:
                u_out[rows, :] = sums(2, i, rows)

        tiles(leaf, leaf_tile, body)

    own_sums(last)
    for i in range(last // 2):
        own_sums(i)
    for off1 in (0, 3, 1, 2):
        near_g.ring2_pass(off1)
    for off1 in (3, 1, 2):
        wt_g.ring2(off1)
    for off1 in (0, 3, 1, 2):
        near_g.to_twin(3, off1)
        near_g.to_twin(1, off1)
    for i in range(last // 2, last):
        own_sums(i)
    key_swap.wait_recv()
    make_one_hot(4, key_in, place.leaf)
    make_one_hot(5, key_in, place.cross[0])
    for off1 in (0, 3, 1, 2):
        near_g.ring2_end(off1)
        near_g.to_twin(2, off1)
    near_g.from_twin()

    def split_partner(index, carry):
        rows = pl.ds(pl.multiple_of(index * 2 * part, 2 * part), 2 * part)
        nq_hi[rows, :], nq_lo[rows, :] = halves(nqp[pl.ds(2 * index, 2)].reshape(2 * part, leaf))
        return carry

    lax.fori_loop(0, nqp.shape[0] // 2, split_partner, 0)

    z_swaps, t_swaps, stores = {}, {}, {}

    def near_chunk(i):
        source_swaps[i].wait_recv()

        def split(rows):
            s_hl[i, rows, :] = beside(s_in[i, rows, :])

        tiles(leaf, LANES, split)
        partial(i)

        def across(rows):
            y_out[i, rows, :] += sums(5, i, rows)

        tiles(leaf, leaf_tile, across)
        sum_swaps[i] = send(y_out.at[i], y_in.at[i], per, (1, i), place.cross)

        def here(rows):
            x[rows, lane(i)] += sums(4, i, rows)

        tiles(leaf, leaf_tile, here)

    def pass_on():
        far_swap.wait_recv()

        def body(rows):
            u_out[rows, :] += w_in[rows, :]

        tiles(leaf, LANES, body)
        return send(u_out, u_in, once, 4, place.mate)

    def weights():
        def split(index, carry):
            count = 2 * inverse.shape[0]
            rows = pl.ds(pl.multiple_of(index * count, 16), count)
            both = wt[pl.ds(2 * index, 2), :, pl.ds(0, leaf + 4 * rank)]
            ws_hi[rows, :], ws_lo[rows, :] = halves(both.reshape(count, leaf + 4 * rank))
            return carry

        lax.fori_loop(0, wt.shape[0] // 2, split, 0)
        for k in range(2):
            v = wt[:, :, pl.ds(leaf + (4 + k) * rank, rank)].reshape(leaf, rank)
            v = v * (1.0 / math.sqrt(2**k * leaf))
            rows = pl.ds(k * rank, rank)
            vt_hi[rows, :], vt_lo[rows, :] = halves(v.T)
        second_v = pl.ds(rank, rank)
        first_w = pl.ds(leaf, 2 * rank)
        m_out[...] = dot3(vt_hi[second_v, :], vt_lo[second_v, :], ws_hi[:, first_w], ws_lo[:, first_w])
        swap = send(m_out, m_in, once, 2, place.mate)
        step = min(256, leaf)
        for k in range(leaf // step):
            block = pl.ds(k * step, step)
            r = dot3(vt_hi[...], vt_lo[...], ws_hi[:, block], ws_lo[:, block])
            b_hi[:, block], b_lo[:, block] = halves(r)
        for k in range((leaf + 4 * rank) // step):
            block = pl.ds(k * step, step)
            sign = 1.0 if k * step < leaf else -1.0

            def body(rows):
                wall_hi[rows, block] = (dot(gt[rows, :], ws_hi[:, block]) * sign).astype(BF16)
                wall_lo[rows, block] = (dot(gt[rows, :], ws_lo[:, block]) * sign).astype(BF16)

            tiles(leaf, leaf_tile, body)
        return swap

    def corrections(swap):
        swap.wait_recv()
        one, two = pl.ds(0, rank), pl.ds(rank, rank)
        k_hi[:, one], k_lo[:, one] = halves(m_out[:, one] + m_in[:, two])
        k_hi[:, two], k_lo[:, two] = halves(m_out[:, two] + m_in[:, one])

    def apply(rows, at, size, value):
        block = pl.ds(at, size)
        return dot_beside(wall_hi[rows, block], wall_lo[rows, block], value)

    def first(i, more=None):
        sum_swaps[i].wait_recv()
        if more is not None:
            more.wait_recv()

        def split(rows):
            whole = x[rows, lane(i)] + y_in[i, rows, :]
            x_hl[rows, :] = beside(whole if more is None else whole + u_in[rows, :])

        tiles(leaf, LANES, split)
        z_out[i] = dot_beside(b_hi[...], b_lo[...], x_hl[...])
        z_swaps[i] = send(z_out.at[i], z_in.at[i], per, (2, i), place.mate)

        def state(rows):
            acc[rows, lane(i)] = apply(rows, 0, leaf, x_hl[...])

        tiles(leaf, leaf_tile, state)

    def second(i):
        z_swaps[i].wait_recv()
        one, two = pl.ds(0, rank), pl.ds(rank, rank)
        c_hl[one, :] = beside(z_in[i, one, :])
        c_hl[two, :] = beside(z_out[i, one, :])
        total = z_out[i, two, :] + z_in[i, two, :] - dot_beside(k_hi[...], k_lo[...], c_hl[...])
        t_out[i] = total
        t_swaps[i] = send(t_out.at[i], t_in.at[i], per, (3, i), place.cross)
        t_hl = beside(total)

        def update(rows):
            acc[rows, lane(i)] += apply(rows, leaf, 2 * rank, c_hl[...]) + apply(
                rows, leaf + 3 * rank, rank, t_hl
            )

        tiles(leaf, leaf_tile, update)

    def third(i):
        t_swaps[i].wait_recv()
        t_hl = beside(t_in[i])

        def update(rows):
            acc[rows, lane(i)] += apply(rows, leaf + 2 * rank, rank, t_hl)

        tiles(leaf, leaf_tile, update)
        stores[i] = pltpu.make_async_copy(acc.at[:, lane(i)], out.at[:, lane(i)], out_sem.at[i])
        stores[i].start()

    near_chunk(0)
    for off1 in (0, 3, 1, 2):
        wt_g.ring2_pass(off1)
        wt_g.to_twin(3, off1)
        wt_g.to_twin(1, off1)
    near_chunk(1)
    mate_sums = pass_on()
    for off1 in (0, 3, 1, 2):
        wt_g.ring2_end(off1)
        wt_g.to_twin(2, off1)
    for i in range(2, last):
        near_chunk(i)
    wt_g.from_twin()
    m_swap = weights()
    first(0)
    corrections(m_swap)
    first(last, mate_sums)
    second(0)
    first(1)
    second(last)
    third(0)
    second(1)
    third(last)
    for i in range(2, last):
        first(i)
        third(i - 1)
        second(i)
    third(last - 1)

    for i in range(chunks):
        stores[i].wait()
    for copy in started:
        copy.wait_send()
    near_g.finish()
    wt_g.finish()


def per_device(
    incident, sources, tree_order, near_quad, near_owner, near_slot, leaf_inverse, basis_v, basis_w
):
    leaf, cols = incident.shape
    near = near_quad.shape[0]
    rank = basis_v.shape[2]
    group = lax.axis_size("col")
    rows = leaf // group
    chunks = cols // LANES
    width = leaf + 6 * rank
    vmem, sem = pltpu.VMEM, pltpu.SemaphoreType.DMA

    def f32(*shape):
        return vmem(shape, F32)

    def pair(*shape):
        return [vmem(shape, BF16), vmem(shape, BF16)]

    scratch = [
        vmem((1, leaf), jnp.int32), vmem((1, near), jnp.int32), vmem((1, near), jnp.int32),
        f32(rows, leaf), f32(2, rows, rank), f32(2, 2, rows, rank),
        f32(near, leaf), f32(leaf, cols), f32(leaf, cols),
        f32(group, near // group, leaf), f32(group, rows, width),
        vmem((8, near), jnp.int32), vmem((8, near), jnp.int32),
        f32(chunks, leaf, LANES), f32(chunks, leaf, LANES), f32(chunks, leaf, LANES),
        f32(chunks, 2 * rank, LANES), f32(chunks, 2 * rank, LANES),
        f32(chunks, rank, LANES), f32(chunks, rank, LANES),
        f32(leaf, LANES), f32(leaf, LANES), f32(leaf, LANES), f32(leaf, LANES),
        f32(rank, 2 * rank), f32(rank, 2 * rank), f32(leaf, cols),
        *pair(near, leaf), vmem((chunks, leaf, 2 * LANES), BF16), vmem((chunks, near, 2 * LANES), BF16),
        vmem((6, leaf, near), BF16), vmem((leaf, leaf), BF16),
        *pair(2 * rank, leaf), *pair(2 * rank, leaf),
        *pair(leaf, leaf + 4 * rank), *pair(leaf, leaf + 4 * rank),
        *pair(rank, 2 * rank), vmem((leaf, 2 * LANES), BF16), vmem((2 * rank, 2 * LANES), BF16),
        sem((2, 32)), sem((2, 32)), sem((4, chunks)), sem((4, chunks)), sem((5,)), sem((5,)),
        sem((9,)), sem((chunks,)),
    ]
    in_any = pl.BlockSpec(memory_space=pl.ANY)
    return pl.pallas_call(
        kernel,
        out_shape=jax.ShapeDtypeStruct((leaf, cols), F32),
        in_specs=[in_any] * 9,
        out_specs=in_any,
        scratch_shapes=scratch,
        compiler_params=pltpu.CompilerParams(
            collective_id=0, has_side_effects=True, vmem_limit_bytes=60 * 1024 * 1024
        ),
        cost_estimate=pl.CostEstimate(flops=15 * 10**9, bytes_accessed=12 * 10**6, transcendentals=0),
    )(
        tree_order, near_owner.reshape(1, near), near_slot.reshape(1, near),
        leaf_inverse, basis_v, basis_w, incident, sources, near_quad,
    )


def solution(mesh):
    placed = (
        P("leaf", "col"),
        P("leaf", "col"),
        P("leaf", None),
        P("leaf", None),
        P("leaf", None),
        P("leaf"),
        P(("leaf", "col"), None),
        P(None, ("leaf", "col"), None),
        P(None, None, ("leaf", "col"), None),
    )
    return jax.shard_map(
        per_device, mesh=mesh, in_specs=placed, out_specs=P("leaf", "col"), check_vma=False
    )
```

```python
import functools
import math

import jax
import jax.numpy as jnp
from jax import lax
from jax.experimental import pallas as pl
from jax.experimental.pallas import tpu as pltpu
from jax.sharding import PartitionSpec as P

MESH = pl.DeviceIdType.MESH
F32 = jnp.float32
BF16 = jnp.bfloat16
LANES = 128
RING = 4


def halves(value):
    top = value.astype(BF16)
    return top, (value - top.astype(F32)).astype(BF16)


def dot(a, b):
    return jnp.dot(a, b, preferred_element_type=F32)


def dot3(a_hi, a_lo, b_hi, b_lo):
    return dot(a_hi, b_hi) + dot(a_hi, b_lo) + dot(a_lo, b_hi)


def beside(value):
    return jnp.concatenate(halves(value), axis=1)


def fold(wide):
    return wide[:, :LANES] + wide[:, LANES:]


def dot_beside(a_hi, a_lo, b):
    return fold(dot(a_hi, b)) + dot(a_lo, b[:, :LANES])


def tiles(count, size, body):
    def step(index, carry):
        body(pl.ds(pl.multiple_of(index * size, size), size))
        return carry

    lax.fori_loop(0, count // size, step, 0)


class Place:
    def __init__(self):
        self.leaf = lax.axis_index("leaf")
        self.col = lax.axis_index("col")
        self.core = self.col % 2
        y = (self.col // 2) % RING
        z = self.col // (2 * RING)
        self.d1 = y * (1 - self.core) + z * self.core
        self.d2 = z * (1 - self.core) + y * self.core
        self.twin = (self.leaf, self.col + 1 - 2 * self.core)
        self.mate = (self.leaf + 1 - 2 * (self.leaf % 2), self.col)
        self.cross = (3 - self.leaf, self.col)
        self.right1 = (self.leaf, self.index(self.core, 0, 1))
        self.left1 = (self.leaf, self.index(self.core, 0, RING - 1))
        self.opposite1 = (self.leaf, self.index(self.core, 0, 2))
        self.far = self.leaf + 2 - 4 * (self.leaf // 2)
        self.right2 = (self.leaf, self.index(self.core, 1, 0))
        self.left2 = (self.leaf, self.index(self.core, RING - 1, 0))

    def index(self, core, off2, off1):
        a, b = (self.d2 + off2) % RING, (self.d1 + off1) % RING
        return (a * 2 * RING + b * 2) * (1 - core) + (b * 2 * RING + a * 2 + 1) * core

    def twin_index(self, off2, off1):
        core = 1 - self.core
        a, b = (self.d1 + off2) % RING, (self.d2 + off1) % RING
        return (a * 2 * RING + b * 2) * (1 - core) + (b * 2 * RING + a * 2 + 1) * core


class Gather:
    def __init__(self, place, buf, send_sem, recv_sem):
        self.p, self.buf, self.ss, self.rs = place, buf, send_sem, recv_sem
        self.started = []

    def piece(self, off2, off1):
        return self.buf.at[self.p.index(self.p.core, off2, off1)]

    def send(self, ref, sem, device):
        copy = pltpu.make_async_remote_copy(
            src_ref=ref, dst_ref=ref, send_sem=self.ss.at[sem], recv_sem=self.rs.at[sem],
            device_id=device, device_id_type=MESH,
        )
        copy.start()
        self.started.append(copy)

    def recv(self, ref, sem):
        pltpu.make_async_remote_copy(
            src_ref=ref, dst_ref=ref, send_sem=self.ss.at[sem], recv_sem=self.rs.at[sem],
            device_id=self.p.twin, device_id_type=MESH,
        ).wait_recv()

    def ring1(self):
        own = self.piece(0, 0)
        self.send(own, 0, self.p.right1)
        self.send(own, 1, self.p.left1)
        self.send(own, 2, self.p.opposite1)

    def ring1_recv(self, off1):
        self.recv(self.piece(0, off1), (3, 1, 2).index(off1))

    def ring2(self, off1):
        self.send(self.piece(0, off1), 4 + off1, self.p.right2)
        self.send(self.piece(0, off1), 8 + off1, self.p.left2)

    def ring2_pass(self, off1):
        self.recv(self.piece(3, off1), 4 + off1)
        if off1 in (0, 1):
            self.send(self.piece(3, off1), 12 + off1, self.p.right2)
        self.recv(self.piece(1, off1), 8 + off1)
        if off1 in (3, 2):
            self.send(self.piece(1, off1), 12 + off1, self.p.left2)

    def ring2_end(self, off1):
        self.recv(self.piece(2, off1), 12 + off1)

    def to_twin(self, off2, off1):
        self.send(self.piece(off2, off1), 16 + 4 * off2 + off1, self.p.twin)

    def from_twin(self):
        for off2 in range(RING):
            for off1 in range(RING):
                ref = self.buf.at[self.p.twin_index(off2, off1)]
                self.recv(ref, 16 + 4 * off2 + off1)

    def finish(self):
        for copy in self.started:
            copy.wait_send()


def kernel(
    tree_any, owner_any, slot_any, inverse_any, basis_v_any, basis_w_any, incident, sources, near_quad, out,
    tree, owner, slot, inverse, basis_v, basis_w,
    nq, s_own, x, nqp, wt, key_out, key_in, s_in, y_out, y_in, z_out, z_in, t_out, t_in, u_out, u_in, w_out, w_in,
    m_out, m_in, acc,
    nq_hi, nq_lo, s_hl, p_hl, oh, gt, vt_hi, vt_lo, b_hi, b_lo, ws_hi, ws_lo, wn_hi, wn_lo,
    k_hi, k_lo, x_hl, c_hl, st_hl, nat,
    gsend, grecv, csend, crecv, osend, orecv, load_sem, out_sem,
):
    leaf, cols = incident.shape
    near = near_quad.shape[0]
    rank = basis_v.shape[2]
    part = nqp.shape[2]
    group = nqp.shape[1]
    chunks = cols // LANES
    last = chunks - 1
    near_tile, leaf_tile = near // 2, leaf // 2
    row_parts = (pl.ds(0, 2 * leaf // 3), pl.ds(2 * leaf // 3, leaf // 3))
    place = Place()
    mine = place.col
    started = []

    def lane(i):
        return pl.ds(i * LANES, LANES)

    pairs = (
        (tree_any, tree), (owner_any, owner), (slot_any, slot), (inverse_any, inverse), (basis_v_any, basis_v),
        (basis_w_any, basis_w), (near_quad, nq), (sources, s_own), (incident, x),
    )
    loads = [pltpu.make_async_copy(src, dst, load_sem.at[i]) for i, (src, dst) in enumerate(pairs)]
    barrier = pltpu.get_barrier_semaphore()
    neighbours = (
        place.mate, place.cross, place.twin, place.right1, place.left1, place.opposite1, place.right2, place.left2
    )
    for device in neighbours:
        pl.semaphore_signal(barrier, inc=1, device_id=device, device_id_type=MESH)
    for copy in loads:
        copy.start()

    def send(src, dst, sems, index, device):
        copy = pltpu.make_async_remote_copy(
            src_ref=src, dst_ref=dst, send_sem=sems[0].at[index], recv_sem=sems[1].at[index],
            device_id=device, device_id_type=MESH,
        )
        copy.start()
        started.append(copy)
        return copy

    near_gs = [Gather(place, nqp.at[h], gsend.at[h], grecv.at[h]) for h in range(2)]
    wt_g = Gather(place, wt, gsend.at[2], grecv.at[2])

    def make_gt(rows):
        number = rows.start + lax.broadcasted_iota(jnp.int32, (rows.size, leaf), 0)
        gt[rows, :] = jnp.where(number == tree[...], 1.0, 0.0).astype(BF16)

    def make_one_hot(which, key, block):
        base = block * leaf

        def body(rows):
            number = base + rows.start + lax.broadcasted_iota(jnp.int32, (rows.size, near), 0)
            oh[which, rows, :] = jnp.where(number == key[0:1, :], 1.0, 0.0).astype(BF16)

        tiles(leaf, LANES, body)

    def split_near(rows):
        nq_hi[rows, :], nq_lo[rows, :] = halves(nq[rows, :])

    def partial_rows(i, rows):
        p_hl[i, rows, :] = beside(dot_beside(nq_hi[rows, :], nq_lo[rows, :], s_hl[i]))

    def partial(i):
        tiles(near, near_tile, lambda rows: partial_rows(i, rows))

    def own_partial(i):
        def body(rows):
            s_hl[i, rows, :] = beside(s_own[rows, lane(i)])

        tiles(leaf, LANES, body)
        partial(i)

    def sums(which, i, rows):
        return fold(dot(oh[which, rows, :], p_hl[i]))

    for copy in loads[:6]:
        copy.wait()
    key_out[...] = owner[...] * leaf + slot[...]
    tiles(leaf, LANES, make_gt)
    nt = (((1,), (1,)), ((), ()))
    top, low = halves(inverse[...])
    wt[mine, :, pl.ds(0, leaf)] = lax.dot_general(
        top, gt[...], nt, preferred_element_type=F32
    ) + lax.dot_general(low, gt[...], nt, preferred_element_type=F32)
    for k in range(4):
        wt[mine, :, pl.ds(leaf + k * rank, rank)] = basis_w[k // 2, k % 2]
    for k in range(2):
        wt[mine, :, pl.ds(leaf + (4 + k) * rank, rank)] = basis_v[k]
    make_one_hot(1, key_out, place.cross[0])
    make_one_hot(3, key_out, place.far)
    loads[6].wait()
    tiles(near, LANES, split_near)
    loads[7].wait()
    own_partial(last)

    pl.semaphore_wait(barrier, len(neighbours))

    once, per = (osend, orecv), (csend, crecv)
    near_swaps = [
        send(
            near_quad.at[pl.ds(pl.multiple_of(h * near // 2 + mine * part, part), part)], nqp.at[h, mine],
            once, h, place.mate,
        )
        for h in range(2)
    ]
    key_swap = send(key_out, key_in, once, 2, place.mate)
    wt_g.ring1()
    wt_g.ring2(0)
    source_swaps = [
        send(sources.at[:, lane(i)], s_in.at[i], per, (0, i), place.mate) for i in range(last)
    ]

    def send_sums(i, part):
        rows = row_parts[part]
        return send(y_out.at[i, rows], y_in.at[i, rows], per, (1 + 3 * part, i), place.cross)

    sum_swaps = {last: []}
    for k in range(2):
        y_out[last, row_parts[k], :] = sums(1, last, row_parts[k])
        sum_swaps[last].append(send_sums(last, k))

    def last_far(rows):
        w_out[rows, :] = sums(3, last, rows)

    tiles(leaf, leaf_tile, last_far)
    far_swap = send(w_out, w_in, once, 3, place.cross)
    make_one_hot(2, key_out, place.mate[0])
    make_one_hot(0, key_out, place.leaf)
    own_partial(0)

    for h in range(2):
        near_swaps[h].wait_recv()
        near_gs[h].ring1()
        near_gs[h].ring2(0)
    wt_g.ring1_recv(3)
    wt_g.ring2(3)
    for g in (*near_gs, wt_g):
        g.to_twin(0, 0)
    for i in range(1, last):
        own_partial(i)
    for g in near_gs:
        for off1 in (3, 1, 2):
            g.ring1_recv(off1)
            g.ring2(off1)
    for g in near_gs:
        g.ring2_pass(0)
        for off1 in (3, 1, 2):
            g.to_twin(0, off1)
    loads[8].wait()

    def own_sums(i):
        def body(rows):
            x[rows, lane(i)] += sums(0, i, rows)
            if i < last:
                y_out[i, rows, :] = sums(1, i, rows)
            else:
                u_out[rows, :] = sums(2, i, rows)

        tiles(leaf, leaf_tile, body)

    own_sums(last)
    for i in range(last // 2):
        own_sums(i)
    wt_g.ring1_recv(1)
    wt_g.ring1_recv(2)
    for g in near_gs:
        for off1 in (3, 1, 2):
            g.ring2_pass(off1)
    wt_g.ring2(1)
    wt_g.ring2(2)
    wt_g.ring2_pass(0)
    wt_g.ring2_pass(3)
    for off1 in (0, 3, 1, 2):
        for g in near_gs:
            g.to_twin(3, off1)
            g.to_twin(1, off1)
    for i in range(last // 2, last):
        own_sums(i)
    key_swap.wait_recv()
    make_one_hot(4, key_in, place.leaf)
    make_one_hot(5, key_in, place.cross[0])
    for g in near_gs:
        for off1 in (0, 3, 1, 2):
            g.ring2_end(off1)
            g.to_twin(2, off1)
    for off1 in (3, 1, 2):
        wt_g.to_twin(0, off1)

    def split_partner(h):
        count = 4 * part

        def body(index, carry):
            rows = pl.ds(pl.multiple_of(h * near // 2 + index * count, count), count)
            block = nqp[h, pl.ds(4 * index, 4)].reshape(count, leaf)
            nq_hi[rows, :], nq_lo[rows, :] = halves(block)
            return carry

        lax.fori_loop(0, group // 4, body, 0)

    z_swaps, t_swaps, stores = {}, {}, {}

    def near_chunk(i):
        source_swaps[i].wait_recv()

        def split(rows):
            s_hl[i, rows, :] = beside(s_in[i, rows, :])

        tiles(leaf, LANES, split)
        if i == 0:
            for h in range(2):
                near_gs[h].from_twin()
                split_partner(h)
                partial_rows(i, pl.ds(h * near // 2, near // 2))
        else:
            partial(i)
        sum_swaps[i] = []
        for k in range(2):
            y_out[i, row_parts[k], :] += sums(5, i, row_parts[k])
            sum_swaps[i].append(send_sums(i, k))

        def here(rows):
            x[rows, lane(i)] += sums(4, i, rows)

        tiles(leaf, leaf_tile, here)

    def pass_on():
        far_swap.wait_recv()

        def body(rows):
            u_out[rows, :] += w_in[rows, :]

        tiles(leaf, LANES, body)
        return send(u_out, u_in, once, 4, place.mate)

    def weights():
        def split(index, carry):
            count = 2 * inverse.shape[0]
            rows = pl.ds(pl.multiple_of(index * count, 16), count)
            both = wt[pl.ds(2 * index, 2), :, pl.ds(0, leaf + 4 * rank)]
            ws_hi[rows, :], ws_lo[rows, :] = halves(both.reshape(count, leaf + 4 * rank))
            return carry

        lax.fori_loop(0, wt.shape[0] // 2, split, 0)
        for k in range(2):
            v = wt[:, :, pl.ds(leaf + (4 + k) * rank, rank)].reshape(leaf, rank)
            v = v * (1.0 / math.sqrt(2**k * leaf))
            rows = pl.ds(k * rank, rank)
            vt_hi[rows, :], vt_lo[rows, :] = halves(v.T)
        second_v = pl.ds(rank, rank)
        first_w = pl.ds(leaf, 2 * rank)
        m_out[...] = dot3(vt_hi[second_v, :], vt_lo[second_v, :], ws_hi[:, first_w], ws_lo[:, first_w])
        mine_m = half_m()
        swap = send(m_out.at[mine_m], m_in.at[mine_m], once, 5, place.mate)
        step = min(256, leaf)
        for k in range(leaf // step):
            block = pl.ds(k * step, step)
            r = dot3(vt_hi[...], vt_lo[...], ws_hi[:, block], ws_lo[:, block])
            b_hi[:, block], b_lo[:, block] = halves(r)
        sibling = pl.ds(leaf + 2 * rank, rank)

        def body(rows):
            wn_hi[rows, :] = dot(gt[rows, :], ws_hi[:, sibling]).astype(BF16)
            wn_lo[rows, :] = dot(gt[rows, :], ws_lo[:, sibling]).astype(BF16)

        tiles(leaf, leaf_tile, body)
        return swap

    def half_m():
        return pl.ds(pl.multiple_of(place.core * (rank // 2), rank // 2), rank // 2)

    def corrections_pass(swap):
        swap.wait_recv()
        ref = m_in.at[half_m()]
        return send(ref, ref, once, 6, place.twin)

    def corrections(swap):
        swap.wait_recv()
        one, two = pl.ds(0, rank), pl.ds(rank, rank)
        k_hi[:, one], k_lo[:, one] = halves(m_out[:, one] + m_in[:, two])
        k_hi[:, two], k_lo[:, two] = halves(m_out[:, two] + m_in[:, one])

    def apply(rows, at, size, value):
        block = pl.ds(at, size)
        return dot_beside(ws_hi[rows, block], ws_lo[rows, block], value)

    def first(i, more=None):
        if more is not None:
            more.wait_recv()
        z = None
        for k, rows in enumerate(row_parts):
            sum_swaps[i][k].wait_recv()
            whole = x[rows, lane(i)] + y_in[i, rows, :]
            x_hl[rows, :] = beside(whole if more is None else whole + u_in[rows, :])
            term = dot_beside(b_hi[:, rows], b_lo[:, rows], x_hl[rows, :])
            z = term if z is None else z + term
        z_out[i] = z
        z_swaps[i] = send(z_out.at[i], z_in.at[i], per, (2, i), place.mate)

        def state(rows):
            acc[rows, lane(i)] = apply(rows, 0, leaf, x_hl[...])

        tiles(leaf, leaf_tile, state)

    def second(i):
        z_swaps[i].wait_recv()
        one, two = pl.ds(0, rank), pl.ds(rank, rank)
        c_hl[one, :] = beside(z_in[i, one, :])
        c_hl[two, :] = beside(z_out[i, one, :])
        total = z_out[i, two, :] + z_in[i, two, :] - dot_beside(k_hi[...], k_lo[...], c_hl[...])
        t_out[i] = total
        t_swaps[i] = send(t_out.at[i], t_in.at[i], per, (3, i), place.cross)
        t_hl = beside(total)

        def update(rows):
            change = apply(rows, leaf, 2 * rank, c_hl[...]) + apply(rows, leaf + 3 * rank, rank, t_hl)
            st_hl[rows, :] = beside(acc[rows, lane(i)] - change)

        tiles(leaf, leaf_tile, update)

        def natural(rows):
            nat[rows, lane(i)] = fold(dot(gt[rows, :], st_hl[...]))

        tiles(leaf, leaf_tile, natural)

    def third(i):
        t_swaps[i].wait_recv()
        t_hl = beside(t_in[i])

        def update(rows):
            nat[rows, lane(i)] -= dot_beside(wn_hi[rows, :], wn_lo[rows, :], t_hl)

        tiles(leaf, leaf_tile, update)
        stores[i] = pltpu.make_async_copy(nat.at[:, lane(i)], out.at[:, lane(i)], out_sem.at[i])
        stores[i].start()

    near_chunk(0)
    for off1 in (1, 2):
        wt_g.ring2_pass(off1)
    for off1 in (0, 3, 1, 2):
        wt_g.to_twin(3, off1)
        wt_g.to_twin(1, off1)
    near_chunk(1)
    mate_sums = pass_on()
    for off1 in (0, 3, 1, 2):
        wt_g.ring2_end(off1)
        wt_g.to_twin(2, off1)
    for i in range(2, last):
        near_chunk(i)
    wt_g.from_twin()
    m_swap = weights()
    first(0)
    first(last, mate_sums)
    m_swap = corrections_pass(m_swap)
    first(1)
    corrections(m_swap)
    second(0)
    second(last)
    second(1)
    third(0)
    for i in range(2, last):
        first(i)
    third(last)
    for i in range(2, last):
        second(i)
    for i in range(1, last):
        third(i)

    for i in range(chunks):
        stores[i].wait()
    for copy in started:
        copy.wait_send()
    for g in (*near_gs, wt_g):
        g.finish()


def per_device(
    incident, sources, tree_order, near_quad, near_owner, near_slot, leaf_inverse, basis_v, basis_w
):
    leaf, cols = incident.shape
    near = near_quad.shape[0]
    rank = basis_v.shape[2]
    group = lax.axis_size("col")
    rows = leaf // group
    chunks = cols // LANES
    width = leaf + 6 * rank
    vmem, sem = pltpu.VMEM, pltpu.SemaphoreType.DMA

    def f32(*shape):
        return vmem(shape, F32)

    def pair(*shape):
        return [vmem(shape, BF16), vmem(shape, BF16)]

    scratch = [
        vmem((1, leaf), jnp.int32), vmem((1, near), jnp.int32), vmem((1, near), jnp.int32),
        f32(rows, leaf), f32(2, rows, rank), f32(2, 2, rows, rank),
        f32(near, leaf), f32(leaf, cols), f32(leaf, cols),
        f32(2, group, near // (2 * group), leaf), f32(group, rows, width),
        vmem((1, near), jnp.int32), vmem((1, near), jnp.int32),
        f32(chunks, leaf, LANES), f32(chunks, leaf, LANES), f32(chunks, leaf, LANES),
        f32(chunks, 2 * rank, LANES), f32(chunks, 2 * rank, LANES),
        f32(chunks, rank, LANES), f32(chunks, rank, LANES),
        f32(leaf, LANES), f32(leaf, LANES), f32(leaf, LANES), f32(leaf, LANES),
        f32(rank, 2 * rank), f32(rank, 2 * rank), f32(leaf, cols),
        *pair(near, leaf), vmem((chunks, leaf, 2 * LANES), BF16), vmem((chunks, near, 2 * LANES), BF16),
        vmem((6, leaf, near), BF16), vmem((leaf, leaf), BF16),
        *pair(2 * rank, leaf), *pair(2 * rank, leaf),
        *pair(leaf, leaf + 4 * rank), *pair(leaf, rank),
        *pair(rank, 2 * rank), vmem((leaf, 2 * LANES), BF16), vmem((2 * rank, 2 * LANES), BF16),
        vmem((leaf, 2 * LANES), BF16), f32(leaf, cols),
        sem((3, 32)), sem((3, 32)), sem((5, chunks)), sem((5, chunks)), sem((7,)), sem((7,)),
        sem((9,)), sem((chunks,)),
    ]
    in_any = pl.BlockSpec(memory_space=pl.ANY)
    return pl.pallas_call(
        kernel,
        out_shape=jax.ShapeDtypeStruct((leaf, cols), F32),
        in_specs=[in_any] * 9,
        out_specs=in_any,
        scratch_shapes=scratch,
        compiler_params=pltpu.CompilerParams(
            collective_id=0, has_side_effects=True, vmem_limit_bytes=60 * 1024 * 1024
        ),
        cost_estimate=pl.CostEstimate(flops=15 * 10**9, bytes_accessed=12 * 10**6, transcendentals=0),
    )(
        tree_order, near_owner.reshape(1, near), near_slot.reshape(1, near),
        leaf_inverse, basis_v, basis_w, incident, sources, near_quad,
    )


def solution(mesh):
    placed = (
        P("leaf", "col"),
        P("leaf", "col"),
        P("leaf", None),
        P("leaf", None),
        P("leaf", None),
        P("leaf"),
        P(("leaf", "col"), None),
        P(None, ("leaf", "col"), None),
        P(None, None, ("leaf", "col"), None),
    )
    return jax.shard_map(
        per_device, mesh=mesh, in_specs=placed, out_specs=P("leaf", "col"), check_vma=False
    )
```

```python
import functools
import math

import jax
import jax.numpy as jnp
from jax import lax
from jax.experimental import pallas as pl
from jax.experimental.pallas import tpu as pltpu
from jax.sharding import PartitionSpec as P

MESH = pl.DeviceIdType.MESH
F32 = jnp.float32
BF16 = jnp.bfloat16
LANES = 128
RING = 4


def halves(value):
    top = value.astype(BF16)
    return top, (value - top.astype(F32)).astype(BF16)


def dot(a, b):
    return jnp.dot(a, b, preferred_element_type=F32)


def dot3(a_hi, a_lo, b_hi, b_lo):
    return dot(a_hi, b_hi) + dot(a_hi, b_lo) + dot(a_lo, b_hi)


def beside(value):
    return jnp.concatenate(halves(value), axis=1)


def fold(wide):
    return wide[:, :LANES] + wide[:, LANES:]


def dot_beside(a_hi, a_lo, b):
    return fold(dot(a_hi, b)) + dot(a_lo, b[:, :LANES])


def tiles(count, size, body):
    def step(index, carry):
        body(pl.ds(pl.multiple_of(index * size, size), size))
        return carry

    lax.fori_loop(0, count // size, step, 0)


class Place:
    def __init__(self):
        self.leaf = lax.axis_index("leaf")
        self.col = lax.axis_index("col")
        self.core = self.col % 2
        y = (self.col // 2) % RING
        z = self.col // (2 * RING)
        self.d1 = y * (1 - self.core) + z * self.core
        self.d2 = z * (1 - self.core) + y * self.core
        self.twin = (self.leaf, self.col + 1 - 2 * self.core)
        self.mate = (self.leaf + 1 - 2 * (self.leaf % 2), self.col)
        self.cross = (3 - self.leaf, self.col)
        self.right1 = (self.leaf, self.index(self.core, 0, 1))
        self.left1 = (self.leaf, self.index(self.core, 0, RING - 1))
        self.opposite1 = (self.leaf, self.index(self.core, 0, 2))
        self.far = (self.leaf + 2 - 4 * (self.leaf // 2), self.col)
        self.right2 = (self.leaf, self.index(self.core, 1, 0))
        self.left2 = (self.leaf, self.index(self.core, RING - 1, 0))

    def index(self, core, off2, off1):
        a, b = (self.d2 + off2) % RING, (self.d1 + off1) % RING
        return (a * 2 * RING + b * 2) * (1 - core) + (b * 2 * RING + a * 2 + 1) * core

    def twin_index(self, off2, off1):
        core = 1 - self.core
        a, b = (self.d1 + off2) % RING, (self.d2 + off1) % RING
        return (a * 2 * RING + b * 2) * (1 - core) + (b * 2 * RING + a * 2 + 1) * core


class Gather:
    def __init__(self, place, buf, send_sem, recv_sem):
        self.p, self.buf, self.ss, self.rs = place, buf, send_sem, recv_sem
        self.started = []

    def piece(self, off2, off1):
        return self.buf.at[self.p.index(self.p.core, off2, off1)]

    def send(self, ref, sem, device):
        copy = pltpu.make_async_remote_copy(
            src_ref=ref, dst_ref=ref, send_sem=self.ss.at[sem], recv_sem=self.rs.at[sem],
            device_id=device, device_id_type=MESH,
        )
        copy.start()
        self.started.append(copy)

    def recv(self, ref, sem):
        pltpu.make_async_remote_copy(
            src_ref=ref, dst_ref=ref, send_sem=self.ss.at[sem], recv_sem=self.rs.at[sem],
            device_id=self.p.twin, device_id_type=MESH,
        ).wait_recv()

    def ring1(self):
        own = self.piece(0, 0)
        self.send(own, 0, self.p.right1)
        self.send(own, 1, self.p.left1)
        self.send(own, 2, self.p.opposite1)

    def ring1_recv(self, off1):
        self.recv(self.piece(0, off1), (3, 1, 2).index(off1))

    def ring2(self, off1):
        self.send(self.piece(0, off1), 4 + off1, self.p.right2)
        self.send(self.piece(0, off1), 8 + off1, self.p.left2)

    def ring2_pass(self, off1):
        self.recv(self.piece(3, off1), 4 + off1)
        if off1 in (0, 1):
            self.send(self.piece(3, off1), 12 + off1, self.p.right2)
        self.recv(self.piece(1, off1), 8 + off1)
        if off1 in (3, 2):
            self.send(self.piece(1, off1), 12 + off1, self.p.left2)

    def ring2_end(self, off1):
        self.recv(self.piece(2, off1), 12 + off1)

    def to_twin(self, off2, off1):
        self.send(self.piece(off2, off1), 16 + 4 * off2 + off1, self.p.twin)

    def from_twin(self):
        for off2 in range(RING):
            for off1 in range(RING):
                ref = self.buf.at[self.p.twin_index(off2, off1)]
                self.recv(ref, 16 + 4 * off2 + off1)

    def finish(self):
        for copy in self.started:
            copy.wait_send()


def kernel(
    tree_any, owner_any, slot_any, inverse_any, basis_v_any, basis_w_any, incident, sources, near_quad, nat,
    tree, owner, slot, inverse, basis_v, basis_w,
    nq, s_own, x, nqp, wt, key_out, key_in, s_in, y_out, y_in, z_out, z_in, t_out, t_in, u_out, u_in, w_out, w_in,
    m_out, m_in, far_in,
    nq_hi, nq_lo, s_hl, p_hl, oh, gt, vt_hi, vt_lo, b_hi, b_lo, ws_hi, ws_lo, wn_hi, wn_lo,
    k_hi, k_lo, x_hl, c_hl, st_hl,
    gsend, grecv, csend, crecv, osend, orecv, load_sem,
):
    leaf, cols = incident.shape
    near = near_quad.shape[0]
    rank = basis_v.shape[2]
    part = nqp.shape[2]
    group = nqp.shape[1]
    chunks = cols // LANES
    last = chunks - 1
    near_tile, leaf_tile = near // 2, leaf // 2
    row_parts = (pl.ds(0, 2 * leaf // 3), pl.ds(2 * leaf // 3, leaf // 3))
    place = Place()
    mine = place.col
    started = []

    def lane(i):
        return pl.ds(i * LANES, LANES)

    pairs = (
        (tree_any, tree), (owner_any, owner), (slot_any, slot), (inverse_any, inverse), (basis_v_any, basis_v),
        (basis_w_any, basis_w), (near_quad, nq), (sources, s_own), (incident, x),
    )
    loads = [pltpu.make_async_copy(src, dst, load_sem.at[i]) for i, (src, dst) in enumerate(pairs)]
    barrier = pltpu.get_barrier_semaphore()
    neighbours = (
        place.mate, place.cross, place.far, place.twin, place.right1, place.left1, place.opposite1, place.right2,
        place.left2,
    )
    for device in neighbours:
        pl.semaphore_signal(barrier, inc=1, device_id=device, device_id_type=MESH)
    for copy in loads:
        copy.start()

    def send(src, dst, sems, index, device):
        copy = pltpu.make_async_remote_copy(
            src_ref=src, dst_ref=dst, send_sem=sems[0].at[index], recv_sem=sems[1].at[index],
            device_id=device, device_id_type=MESH,
        )
        copy.start()
        started.append(copy)
        return copy

    near_gs = [Gather(place, nqp.at[h], gsend.at[h], grecv.at[h]) for h in range(2)]
    wt_g = Gather(place, wt, gsend.at[2], grecv.at[2])

    def make_gt(rows):
        number = rows.start + lax.broadcasted_iota(jnp.int32, (rows.size, leaf), 0)
        gt[rows, :] = jnp.where(number == tree[...], 1.0, 0.0).astype(BF16)

    def make_one_hot(which, key, block):
        base = block * leaf

        def body(rows):
            number = base + rows.start + lax.broadcasted_iota(jnp.int32, (rows.size, near), 0)
            oh[which, rows, :] = jnp.where(number == key[0:1, :], 1.0, 0.0).astype(BF16)

        tiles(leaf, LANES, body)

    def split_near(rows):
        nq_hi[rows, :], nq_lo[rows, :] = halves(nq[rows, :])

    def partial_rows(i, rows):
        p_hl[i, rows, :] = beside(dot_beside(nq_hi[rows, :], nq_lo[rows, :], s_hl[i]))

    def partial(i):
        tiles(near, near_tile, lambda rows: partial_rows(i, rows))

    def own_partial(i):
        def body(rows):
            s_hl[i, rows, :] = beside(s_own[rows, lane(i)])

        tiles(leaf, LANES, body)
        partial(i)

    def sums(which, i, rows):
        return fold(dot(oh[which, rows, :], p_hl[i]))

    for copy in loads[:6]:
        copy.wait()
    key_out[...] = owner[...] * leaf + slot[...]
    tiles(leaf, LANES, make_gt)
    nt = (((1,), (1,)), ((), ()))
    top, low = halves(inverse[...])
    wt[mine, :, pl.ds(0, leaf)] = lax.dot_general(
        top, gt[...], nt, preferred_element_type=F32
    ) + lax.dot_general(low, gt[...], nt, preferred_element_type=F32)
    for k in range(4):
        wt[mine, :, pl.ds(leaf + k * rank, rank)] = basis_w[k // 2, k % 2]
    for k in range(2):
        wt[mine, :, pl.ds(leaf + (4 + k) * rank, rank)] = basis_v[k]
    make_one_hot(1, key_out, place.cross[0])
    make_one_hot(3, key_out, place.far[0])
    loads[6].wait()
    tiles(near, LANES, split_near)
    loads[7].wait()
    own_partial(last)

    pl.semaphore_wait(barrier, len(neighbours))

    once, per = (osend, orecv), (csend, crecv)
    near_swaps = [
        send(
            near_quad.at[pl.ds(pl.multiple_of(h * near // 2 + mine * part, part), part)], nqp.at[h, mine],
            once, h, place.mate,
        )
        for h in range(2)
    ]
    key_swap = send(key_out, key_in, once, 2, place.mate)
    wt_g.ring1()
    source_swaps = [
        send(sources.at[:, lane(i)], s_in.at[i], per, (0, i), place.mate) for i in range(last)
    ]

    def send_sums(i, part):
        rows = row_parts[part]
        return send(y_out.at[i, rows], y_in.at[i, rows], per, (1 + 3 * part, i), place.cross)

    sum_swaps = {last: []}
    for k in range(2):
        y_out[last, row_parts[k], :] = sums(1, last, row_parts[k])
        sum_swaps[last].append(send_sums(last, k))

    def last_far(rows):
        w_out[rows, :] = sums(3, last, rows)

    tiles(leaf, leaf_tile, last_far)
    far_swap = send(w_out, w_in, once, 3, place.cross)
    make_one_hot(2, key_out, place.mate[0])
    make_one_hot(0, key_out, place.leaf)
    own_partial(0)
    loads[8].wait()

    def own_sums(i):
        def body(rows):
            x[rows, lane(i)] += sums(0, i, rows)
            if i < last:
                y_out[i, rows, :] = sums(1, i, rows)
            else:
                u_out[rows, :] = sums(2, i, rows)

        tiles(leaf, leaf_tile, body)

    for g, swap in zip(near_gs, near_swaps):
        swap.wait_recv()
        g.ring1()
        g.ring2(0)
        g.to_twin(0, 0)
    own_partial(1)
    own_sums(last)
    for g in near_gs:
        for off1 in (3, 1, 2):
            g.ring1_recv(off1)
            g.ring2(off1)
        g.ring2_pass(0)
    for g in near_gs:
        for off1 in (3, 1, 2):
            g.to_twin(0, off1)
    own_sums(0)
    for i in range(2, last):
        own_partial(i)
    for off1 in (3, 1, 2):
        near_gs[0].ring2_pass(off1)
    own_sums(1)
    for off1 in (3, 1, 2):
        near_gs[1].ring2_pass(off1)
    wt_g.ring2(0)
    for off1 in (3, 1, 2):
        wt_g.ring1_recv(off1)
        wt_g.ring2(off1)
    for g in near_gs:
        for off1 in (0, 3, 1, 2):
            g.to_twin(3, off1)
            g.to_twin(1, off1)
    key_swap.wait_recv()
    make_one_hot(5, key_in, place.cross[0])
    make_one_hot(4, key_in, place.leaf)
    for off1 in (0, 3, 1, 2):
        near_gs[0].ring2_end(off1)
        near_gs[0].to_twin(2, off1)
    for i in range(2, last):
        own_sums(i)
    for off1 in (0, 3, 1, 2):
        near_gs[1].ring2_end(off1)
        near_gs[1].to_twin(2, off1)
    for off1 in (0, 3, 1, 2):
        wt_g.to_twin(0, off1)

    def split_partner(h):
        count = 4 * part

        def body(index, carry):
            rows = pl.ds(pl.multiple_of(h * near // 2 + index * count, count), count)
            block = nqp[h, pl.ds(4 * index, 4)].reshape(count, leaf)
            nq_hi[rows, :], nq_lo[rows, :] = halves(block)
            return carry

        lax.fori_loop(0, group // 4, body, 0)

    z_swaps, t_swaps = {}, {}

    def near_chunk(i):
        source_swaps[i].wait_recv()

        def split(rows):
            s_hl[i, rows, :] = beside(s_in[i, rows, :])

        tiles(leaf, LANES, split)
        if i == 0:
            for h in range(2):
                near_gs[h].from_twin()
                split_partner(h)
                partial_rows(i, pl.ds(h * near // 2, near // 2))
        else:
            partial(i)
        sum_swaps[i] = []
        for k in range(2):
            y_out[i, row_parts[k], :] += sums(5, i, row_parts[k])
            sum_swaps[i].append(send_sums(i, k))

        def here(rows):
            x[rows, lane(i)] += sums(4, i, rows)

        tiles(leaf, leaf_tile, here)

    def pass_on():
        far_swap.wait_recv()

        def body(rows):
            u_out[rows, :] += w_in[rows, :]

        tiles(leaf, LANES, body)
        return send(u_out, u_in, once, 4, place.mate)

    def weights():
        def split(index, carry):
            count = 2 * inverse.shape[0]
            rows = pl.ds(pl.multiple_of(index * count, 16), count)
            both = wt[pl.ds(2 * index, 2), :, pl.ds(0, leaf + 4 * rank)]
            ws_hi[rows, :], ws_lo[rows, :] = halves(both.reshape(count, leaf + 4 * rank))
            return carry

        lax.fori_loop(0, wt.shape[0] // 2, split, 0)
        for k in range(2):
            v = wt[:, :, pl.ds(leaf + (4 + k) * rank, rank)].reshape(leaf, rank)
            v = v * (1.0 / math.sqrt(2**k * leaf))
            rows = pl.ds(k * rank, rank)
            vt_hi[rows, :], vt_lo[rows, :] = halves(v.T)
        second_v = pl.ds(rank, rank)
        first_w = pl.ds(leaf, 2 * rank)
        m_out[...] = dot3(vt_hi[second_v, :], vt_lo[second_v, :], ws_hi[:, first_w], ws_lo[:, first_w])
        mine_m = half_m()
        swap = send(m_out.at[mine_m], m_in.at[mine_m], once, 5, place.mate)
        step = min(256, leaf)
        for k in range(leaf // step):
            block = pl.ds(k * step, step)
            r = dot3(vt_hi[...], vt_lo[...], ws_hi[:, block], ws_lo[:, block])
            b_hi[:, block], b_lo[:, block] = halves(r)
        for k in range(2):
            block, source = pl.ds(2 * k * rank, 2 * rank), pl.ds(leaf + 2 * k * rank, 2 * rank)

            def body(rows):
                wn_hi[rows, block] = dot(gt[rows, :], ws_hi[:, source]).astype(BF16)
                wn_lo[rows, block] = dot(gt[rows, :], ws_lo[:, source]).astype(BF16)

            tiles(leaf, leaf_tile, body)
        return swap

    def half_m():
        return pl.ds(pl.multiple_of(place.core * (rank // 2), rank // 2), rank // 2)

    def corrections_pass(swap):
        swap.wait_recv()
        ref = m_in.at[half_m()]
        return send(ref, ref, once, 6, place.twin)

    def corrections(swap):
        swap.wait_recv()
        one, two = pl.ds(0, rank), pl.ds(rank, rank)
        k_hi[:, one], k_lo[:, one] = halves(m_out[:, one] + m_in[:, two])
        k_hi[:, two], k_lo[:, two] = halves(m_out[:, two] + m_in[:, one])

    one, two = pl.ds(0, rank), pl.ds(rank, rank)
    state_columns = pl.ds(0, leaf)

    def correct(rows, i, at, size):
        block = pl.ds(at * rank, size * rank)
        nat[rows, lane(i)] -= dot_beside(wn_hi[rows, block], wn_lo[rows, block], c_hl[block, :])

    def first(i, more=None):
        if more is not None:
            more.wait_recv()
        z = None
        for k, rows in enumerate(row_parts):
            sum_swaps[i][k].wait_recv()
            whole = x[rows, lane(i)] + y_in[i, rows, :]
            x_hl[rows, :] = beside(whole if more is None else whole + u_in[rows, :])
            term = dot_beside(b_hi[:, rows], b_lo[:, rows], x_hl[rows, :])
            z = term if z is None else z + term
        z_out[i] = z
        if i == direct:
            own = beside(z_out[i, one, :])
            z_out[i, two, :] = z_out[i, two, :] - dot_beside(k_hi[:, two], k_lo[:, two], own)
            far_swaps.append(send(z_out.at[i, two], far_in, once, 7, place.far))
            t_swaps[i] = send(z_out.at[i, two], t_in.at[i], per, (3, i), place.cross)
        z_swaps[i] = send(z_out.at[i], z_in.at[i], per, (2, i), place.mate)

        def state(rows):
            st_hl[rows, :] = beside(dot_beside(ws_hi[rows, state_columns], ws_lo[rows, state_columns], x_hl[...]))

        tiles(leaf, leaf_tile, state)

        def natural(rows):
            nat[rows, lane(i)] = fold(dot(gt[rows, :], st_hl[...]))

        tiles(leaf, leaf_tile, natural)

    def second(i):
        z_swaps[i].wait_recv()
        c_hl[one, :] = beside(z_in[i, one, :])
        c_hl[two, :] = beside(z_out[i, one, :])
        both = pl.ds(0, 2 * rank)
        total = z_out[i, two, :] + z_in[i, two, :] - dot_beside(k_hi[...], k_lo[...], c_hl[both, :])
        t_out[i] = total
        t_swaps[i] = send(t_out.at[i], t_in.at[i], per, (3, i), place.cross)
        c_hl[pl.ds(3 * rank, rank), :] = beside(total)

        def update(rows):
            correct(rows, i, 0, 2)
            correct(rows, i, 3, 1)

        tiles(leaf, leaf_tile, update)

    def third(i):
        t_swaps[i].wait_recv()
        c_hl[pl.ds(2 * rank, rank), :] = beside(t_in[i])
        tiles(leaf, leaf_tile, lambda rows: correct(rows, i, 2, 1))

    def at_once(i):
        z_swaps[i].wait_recv()
        c_hl[one, :] = beside(z_in[i, one, :])
        c_hl[two, :] = beside(z_out[i, one, :])
        c_hl[pl.ds(3 * rank, rank), :] = beside(z_out[i, two, :] + z_in[i, two, :])
        t_swaps[i].wait_recv()
        far_swaps[0].wait_recv()
        c_hl[pl.ds(2 * rank, rank), :] = beside(t_in[i] + far_in[...])
        tiles(leaf, leaf_tile, lambda rows: correct(rows, i, 0, 4))

    direct = last - 1
    far_swaps = []
    near_chunk(0)
    near_chunk(1)
    mate_sums = pass_on()
    for off1 in (0, 3, 1, 2):
        wt_g.ring2_pass(off1)
    for off1 in (0, 3, 1, 2):
        wt_g.to_twin(3, off1)
        wt_g.to_twin(1, off1)
    for i in range(2, last):
        near_chunk(i)
    for off1 in (0, 3, 1, 2):
        wt_g.ring2_end(off1)
        wt_g.to_twin(2, off1)
    wt_g.from_twin()
    m_swap = weights()
    first(0)
    first(last, mate_sums)
    m_swap = corrections_pass(m_swap)
    first(1)
    corrections(m_swap)
    for i in (0, last, 1):
        second(i)
    first(direct)
    for i in (0, last, 1):
        third(i)
    at_once(direct)

    for copy in started:
        copy.wait_send()
    for g in (*near_gs, wt_g):
        g.finish()


def hand_over(value, out, out_sem):
    count = out_sem.shape[0]
    size = value.shape[0] // count
    copies = [
        pltpu.make_async_copy(value.at[pl.ds(i * size, size)], out.at[pl.ds(i * size, size)], out_sem.at[i])
        for i in range(count)
    ]
    for copy in copies:
        copy.start()
    for copy in copies:
        copy.wait()


def per_device(
    incident, sources, tree_order, near_quad, near_owner, near_slot, leaf_inverse, basis_v, basis_w
):
    leaf, cols = incident.shape
    near = near_quad.shape[0]
    rank = basis_v.shape[2]
    group = lax.axis_size("col")
    rows = leaf // group
    chunks = cols // LANES
    width = leaf + 6 * rank
    vmem, sem = pltpu.VMEM, pltpu.SemaphoreType.DMA

    def f32(*shape):
        return vmem(shape, F32)

    def pair(*shape):
        return [vmem(shape, BF16), vmem(shape, BF16)]

    scratch = [
        vmem((1, leaf), jnp.int32), vmem((1, near), jnp.int32), vmem((1, near), jnp.int32),
        f32(rows, leaf), f32(2, rows, rank), f32(2, 2, rows, rank),
        f32(near, leaf), f32(leaf, cols), f32(leaf, cols),
        f32(2, group, near // (2 * group), leaf), f32(group, rows, width),
        vmem((1, near), jnp.int32), vmem((1, near), jnp.int32),
        f32(chunks, leaf, LANES), f32(chunks, leaf, LANES), f32(chunks, leaf, LANES),
        f32(chunks, 2 * rank, LANES), f32(chunks, 2 * rank, LANES),
        f32(chunks, rank, LANES), f32(chunks, rank, LANES),
        f32(leaf, LANES), f32(leaf, LANES), f32(leaf, LANES), f32(leaf, LANES),
        f32(rank, 2 * rank), f32(rank, 2 * rank), f32(rank, LANES),
        *pair(near, leaf), vmem((chunks, leaf, 2 * LANES), BF16), vmem((chunks, near, 2 * LANES), BF16),
        vmem((6, leaf, near), BF16), vmem((leaf, leaf), BF16),
        *pair(2 * rank, leaf), *pair(2 * rank, leaf),
        *pair(leaf, leaf + 4 * rank), *pair(leaf, 4 * rank),
        *pair(rank, 2 * rank), vmem((leaf, 2 * LANES), BF16), vmem((4 * rank, 2 * LANES), BF16),
        vmem((leaf, 2 * LANES), BF16),
        sem((3, 32)), sem((3, 32)), sem((5, chunks)), sem((5, chunks)), sem((8,)), sem((8,)),
        sem((9,)),
    ]
    in_any = pl.BlockSpec(memory_space=pl.ANY)
    solved = pl.pallas_call(
        kernel,
        out_shape=pltpu.VMEM((leaf, cols), F32),
        in_specs=[in_any] * 9,
        out_specs=pl.BlockSpec(memory_space=pltpu.VMEM),
        scratch_shapes=scratch,
        compiler_params=pltpu.CompilerParams(
            collective_id=0, has_side_effects=True, vmem_limit_bytes=54 * 1024 * 1024
        ),
        cost_estimate=pl.CostEstimate(flops=15 * 10**9, bytes_accessed=12 * 10**6, transcendentals=0),
    )(
        tree_order, near_owner.reshape(1, near), near_slot.reshape(1, near),
        leaf_inverse, basis_v, basis_w, incident, sources, near_quad,
    )
    return pl.pallas_call(
        hand_over,
        out_shape=jax.ShapeDtypeStruct((leaf, cols), F32),
        in_specs=[pl.BlockSpec(memory_space=pltpu.VMEM)],
        out_specs=in_any,
        scratch_shapes=[sem((chunks,))],
    )(solved)


def solution(mesh):
    placed = (
        P("leaf", "col"),
        P("leaf", "col"),
        P("leaf", None),
        P("leaf", None),
        P("leaf", None),
        P("leaf"),
        P(("leaf", "col"), None),
        P(None, ("leaf", "col"), None),
        P(None, None, ("leaf", "col"), None),
    )
    return jax.shard_map(
        per_device, mesh=mesh, in_specs=placed, out_specs=P("leaf", "col"), check_vma=False
    )
```

```python
import functools
import math

import jax
import jax.numpy as jnp
from jax import lax
from jax.experimental import pallas as pl
from jax.experimental.pallas import tpu as pltpu
from jax.sharding import PartitionSpec as P

MESH = pl.DeviceIdType.MESH
F32 = jnp.float32
BF16 = jnp.bfloat16
LANES = 128
RING = 4


def halves(value):
    top = value.astype(BF16)
    return top, (value - top.astype(F32)).astype(BF16)


def dot(a, b):
    return jnp.dot(a, b, preferred_element_type=F32)


def dot3(a_hi, a_lo, b_hi, b_lo):
    return dot(a_hi, b_hi) + dot(a_hi, b_lo) + dot(a_lo, b_hi)


def beside(value):
    return jnp.concatenate(halves(value), axis=1)


def fold(wide):
    return wide[:, :LANES] + wide[:, LANES:]


def dot_beside(a_hi, a_lo, b):
    return fold(dot(a_hi, b)) + dot(a_lo, b[:, :LANES])


def tiles(count, size, body):
    def step(index, carry):
        body(pl.ds(pl.multiple_of(index * size, size), size))
        return carry

    lax.fori_loop(0, count // size, step, 0)


class Place:
    def __init__(self):
        self.leaf = lax.axis_index("leaf")
        self.col = lax.axis_index("col")
        self.core = self.col % 2
        y = (self.col // 2) % RING
        z = self.col // (2 * RING)
        self.d1 = y * (1 - self.core) + z * self.core
        self.d2 = z * (1 - self.core) + y * self.core
        self.twin = (self.leaf, self.col + 1 - 2 * self.core)
        self.mate = (self.leaf + 1 - 2 * (self.leaf % 2), self.col)
        self.cross = (3 - self.leaf, self.col)
        self.right1 = self.device(0, 1)
        self.left1 = self.device(0, RING - 1)
        self.opposite1 = self.device(0, 2)
        self.far = (self.leaf + 2 - 4 * (self.leaf // 2), self.col)
        self.right2 = self.device(1, 0)
        self.left2 = self.device(RING - 1, 0)

    def device(self, off2, off1):
        a, b, core = (self.d2 + off2) % RING, (self.d1 + off1) % RING, self.core
        return self.leaf, (a * 2 * RING + b * 2) * (1 - core) + (b * 2 * RING + a * 2 + 1) * core

    def group(self, off2):
        return (self.core * RING + (self.d2 + off2) % RING) * RING

    def twin_group(self, off2):
        return ((1 - self.core) * RING + (self.d1 + off2) % RING) * RING

    def index(self, off2, off1):
        return self.group(off2) + (self.d1 + off1) % RING

    def twin_index(self, off2, off1):
        return self.twin_group(off2) + (self.d2 + off1) % RING


class Gather:
    def __init__(self, place, buf, send_sem, recv_sem):
        self.p, self.buf, self.ss, self.rs = place, buf, send_sem, recv_sem
        self.started = []

    def piece(self, off2, off1):
        return self.buf.at[self.p.index(off2, off1)]

    def send(self, ref, sem, device):
        copy = pltpu.make_async_remote_copy(
            src_ref=ref, dst_ref=ref, send_sem=self.ss.at[sem], recv_sem=self.rs.at[sem],
            device_id=device, device_id_type=MESH,
        )
        copy.start()
        self.started.append(copy)

    def recv(self, ref, sem):
        pltpu.make_async_remote_copy(
            src_ref=ref, dst_ref=ref, send_sem=self.ss.at[sem], recv_sem=self.rs.at[sem],
            device_id=self.p.twin, device_id_type=MESH,
        ).wait_recv()

    def ring1(self):
        own = self.piece(0, 0)
        self.send(own, 0, self.p.right1)
        self.send(own, 1, self.p.left1)
        self.send(own, 2, self.p.opposite1)

    def ring1_recv(self, off1):
        self.recv(self.piece(0, off1), (3, 1, 2).index(off1))

    def ring2(self, off1):
        self.send(self.piece(0, off1), 4 + off1, self.p.right2)
        self.send(self.piece(0, off1), 8 + off1, self.p.left2)

    def ring2_pass(self, off1):
        self.recv(self.piece(3, off1), 4 + off1)
        if off1 in (0, 1):
            self.send(self.piece(3, off1), 12 + off1, self.p.right2)
        self.recv(self.piece(1, off1), 8 + off1)
        if off1 in (3, 2):
            self.send(self.piece(1, off1), 12 + off1, self.p.left2)

    def ring2_end(self, off1):
        self.recv(self.piece(2, off1), 12 + off1)

    def to_twin(self, off2):
        self.send(self.buf.at[pl.ds(self.p.group(off2), RING)], 16 + off2, self.p.twin)

    def end_to_twin(self, off1):
        self.ring2_end(off1)
        self.send(self.piece(2, off1), 20 + off1, self.p.twin)

    def from_twin(self):
        for off2 in (0, 3, 1):
            self.recv(self.buf.at[pl.ds(self.p.twin_group(off2), RING)], 16 + off2)
        for off1 in (0, 3, 1, 2):
            self.recv(self.buf.at[self.p.twin_index(2, off1)], 20 + off1)

    def finish(self):
        for copy in self.started:
            copy.wait_send()


def kernel(
    tree_any, owner_any, slot_any, inverse_any, basis_v_any, basis_w_any, incident, sources, near_quad, nat,
    tree, owner, slot, inverse, basis_v, basis_w,
    nq, s_own, x, nqp, wt, key_out, key_in, s_in, y_out, y_in, z_out, z_in, t_out, t_in, u_out, u_in, w_out, w_in,
    m_out, m_in, far_in,
    nq_hi, nq_lo, s_hl, p_hl, oh, gt, vt_hi, vt_lo, b_hi, b_lo, ws_hi, ws_lo, wn_hi, wn_lo,
    k_hi, k_lo, x_hl, c_hl, st_hl, v_all,
    gsend, grecv, csend, crecv, osend, orecv, load_sem,
):
    leaf, cols = incident.shape
    near = near_quad.shape[0]
    rank = basis_v.shape[2]
    part = nqp.shape[2]
    group = nqp.shape[1]
    chunks = cols // LANES
    last = chunks - 1
    near_tile, leaf_tile = near // 2, leaf // 2
    row_parts = (pl.ds(0, 2 * leaf // 3), pl.ds(2 * leaf // 3, leaf // 3))
    place = Place()
    mine = place.index(0, 0)
    started = []

    def lane(i):
        return pl.ds(i * LANES, LANES)

    pairs = (
        (tree_any, tree), (owner_any, owner), (slot_any, slot), (inverse_any, inverse), (basis_v_any, basis_v),
        (basis_w_any, basis_w), (near_quad, nq), (sources, s_own), (incident, x),
    )
    loads = [pltpu.make_async_copy(src, dst, load_sem.at[i]) for i, (src, dst) in enumerate(pairs)]
    barrier = pltpu.get_barrier_semaphore()
    neighbours = (
        place.mate, place.cross, place.far, place.twin, place.right1, place.left1, place.opposite1, place.right2,
        place.left2,
    )
    for device in neighbours:
        pl.semaphore_signal(barrier, inc=1, device_id=device, device_id_type=MESH)
    for copy in loads:
        copy.start()

    def send(src, dst, sems, index, device):
        copy = pltpu.make_async_remote_copy(
            src_ref=src, dst_ref=dst, send_sem=sems[0].at[index], recv_sem=sems[1].at[index],
            device_id=device, device_id_type=MESH,
        )
        copy.start()
        started.append(copy)
        return copy

    near_gs = [Gather(place, nqp.at[h], gsend.at[h], grecv.at[h]) for h in range(2)]
    wt_g = Gather(place, wt, gsend.at[2], grecv.at[2])

    def make_gt(rows):
        number = rows.start + lax.broadcasted_iota(jnp.int32, (rows.size, leaf), 0)
        gt[rows, :] = jnp.where(number == tree[...], 1.0, 0.0).astype(BF16)

    def make_one_hot(which, key, block):
        base = block * leaf

        def body(rows):
            number = base + rows.start + lax.broadcasted_iota(jnp.int32, (rows.size, near), 0)
            oh[which, rows, :] = jnp.where(number == key[0:1, :], 1.0, 0.0).astype(BF16)

        tiles(leaf, LANES, body)

    def split_near(rows):
        nq_hi[rows, :], nq_lo[rows, :] = halves(nq[rows, :])

    def partial_rows(i, rows):
        p_hl[i, rows, :] = beside(dot_beside(nq_hi[rows, :], nq_lo[rows, :], s_hl[i]))

    def partial(i):
        tiles(near, near_tile, lambda rows: partial_rows(i, rows))

    def own_partial(i):
        def body(rows):
            s_hl[i, rows, :] = beside(s_own[rows, lane(i)])

        tiles(leaf, LANES, body)
        partial(i)

    def sums(which, i, rows):
        return fold(dot(oh[which, rows, :], p_hl[i]))

    for copy in loads[:6]:
        copy.wait()
    key_out[...] = owner[...] * leaf + slot[...]
    tiles(leaf, LANES, make_gt)
    nt = (((1,), (1,)), ((), ()))
    top, low = halves(inverse[...])
    wt[mine, :, pl.ds(0, leaf)] = lax.dot_general(
        top, gt[...], nt, preferred_element_type=F32
    ) + lax.dot_general(low, gt[...], nt, preferred_element_type=F32)
    for k in range(4):
        wt[mine, :, pl.ds(leaf + k * rank, rank)] = basis_w[k // 2, k % 2]
    for k in range(2):
        wt[mine, :, pl.ds(leaf + (4 + k) * rank, rank)] = basis_v[k]
    make_one_hot(1, key_out, place.cross[0])
    make_one_hot(3, key_out, place.far[0])
    loads[6].wait()
    tiles(near, LANES, split_near)
    loads[7].wait()
    own_partial(last)

    pl.semaphore_wait(barrier, len(neighbours))

    once, per = (osend, orecv), (csend, crecv)
    near_swaps = [
        send(
            near_quad.at[pl.ds(pl.multiple_of(h * near // 2 + mine * part, part), part)], nqp.at[h, mine],
            once, h, place.mate,
        )
        for h in range(2)
    ]
    key_swap = send(key_out, key_in, once, 2, place.mate)
    wt_g.ring1()
    source_swaps = [
        send(sources.at[:, lane(i)], s_in.at[i], per, (0, i), place.mate) for i in range(last)
    ]

    def send_sums(i, part):
        rows = row_parts[part]
        return send(y_out.at[i, rows], y_in.at[i, rows], per, (1 + 3 * part, i), place.cross)

    sum_swaps = {last: []}
    for k in range(2):
        y_out[last, row_parts[k], :] = sums(1, last, row_parts[k])
        sum_swaps[last].append(send_sums(last, k))

    def last_far(rows):
        w_out[rows, :] = sums(3, last, rows)

    tiles(leaf, leaf_tile, last_far)
    far_swap = send(w_out, w_in, once, 3, place.cross)
    own_partial(0)
    loads[8].wait()

    def own_sums(i):
        def body(rows):
            x[rows, lane(i)] += sums(0, i, rows)
            if i < last:
                y_out[i, rows, :] = sums(1, i, rows)
            else:
                u_out[rows, :] = sums(2, i, rows)

        tiles(leaf, leaf_tile, body)

    def split_swapped(i):
        source_swaps[i].wait_recv()

        def body(rows):
            s_hl[i, rows, :] = beside(s_in[i, rows, :])

        tiles(leaf, LANES, body)

    for g, swap in zip(near_gs, near_swaps):
        swap.wait_recv()
        g.ring1()
        g.ring2(0)
    make_one_hot(0, key_out, place.leaf)
    own_sums(0)
    make_one_hot(2, key_out, place.mate[0])
    for g in near_gs:
        for off1 in (3, 1, 2):
            g.ring1_recv(off1)
            g.ring2(off1)
        g.ring2_pass(0)
    for g in near_gs:
        g.to_twin(0)
    own_partial(1)
    for g in near_gs:
        for off1 in (3, 1, 2):
            g.ring2_pass(off1)
    wt_g.ring2(0)
    for off1 in (3, 1, 2):
        wt_g.ring1_recv(off1)
        wt_g.ring2(off1)
    for g in near_gs:
        g.to_twin(3)
        g.to_twin(1)
    key_swap.wait_recv()
    make_one_hot(5, key_in, place.cross[0])
    split_swapped(0)
    for off1 in (0, 3, 1, 2):
        near_gs[0].end_to_twin(off1)
    for i in range(2, last):
        own_partial(i)
    for off1 in (0, 3, 1, 2):
        near_gs[1].end_to_twin(off1)
    make_one_hot(4, key_in, place.leaf)
    wt_g.to_twin(0)

    def split_partner(h):
        count = 4 * part

        def body(index, carry):
            rows = pl.ds(pl.multiple_of(h * near // 2 + index * count, count), count)
            block = nqp[h, pl.ds(4 * index, 4)].reshape(count, leaf)
            nq_hi[rows, :], nq_lo[rows, :] = halves(block)
            return carry

        lax.fori_loop(0, group // 4, body, 0)

    z_swaps, t_swaps = {}, {}

    def near_chunk(i):
        if i > 0:
            split_swapped(i)
        if i == 0:
            for h in range(2):
                near_gs[h].from_twin()
                split_partner(h)
                partial_rows(i, pl.ds(h * near // 2, near // 2))
        else:
            partial(i)
        sum_swaps[i] = []
        for k in range(2):
            y_out[i, row_parts[k], :] += sums(5, i, row_parts[k])
            sum_swaps[i].append(send_sums(i, k))

        def here(rows):
            x[rows, lane(i)] += sums(4, i, rows)

        tiles(leaf, leaf_tile, here)

    def pass_on():
        far_swap.wait_recv()

        def body(rows):
            u_out[rows, :] += w_in[rows, :]

        tiles(leaf, LANES, body)
        return send(u_out, u_in, once, 4, place.mate)

    def weights():
        count = inverse.shape[0]
        scale = [1.0 / math.sqrt(2**k * leaf) for k in range(2)]

        def split(pair, carry):
            rows = pl.ds(pl.multiple_of(pair * 2 * count, 16), 2 * count)
            other = RING * RING + (pair % RING) * RING + pair // RING
            both = jnp.concatenate([wt[pair], wt[other]], axis=0)
            ws_hi[rows, :], ws_lo[rows, :] = halves(both[:, : leaf + 4 * rank])
            for k in range(2):
                at = leaf + (4 + k) * rank
                v_all[rows, pl.ds(k * rank, rank)] = both[:, at : at + rank] * scale[k]
            return carry

        lax.fori_loop(0, RING * RING, split, 0)
        vt_hi[...], vt_lo[...] = halves(v_all[...].T)
        second_v = pl.ds(rank, rank)
        first_w = pl.ds(leaf, 2 * rank)
        m_out[...] = dot3(vt_hi[second_v, :], vt_lo[second_v, :], ws_hi[:, first_w], ws_lo[:, first_w])
        mine_m = half_m()
        swap = send(m_out.at[mine_m], m_in.at[mine_m], once, 5, place.mate)
        step = min(256, leaf)
        for k in range(leaf // step):
            block = pl.ds(k * step, step)
            r = dot3(vt_hi[...], vt_lo[...], ws_hi[:, block], ws_lo[:, block])
            b_hi[:, block], b_lo[:, block] = halves(r)
        for k in range(2):
            block, source = pl.ds(2 * k * rank, 2 * rank), pl.ds(leaf + 2 * k * rank, 2 * rank)

            def body(rows):
                wn_hi[rows, block] = dot(gt[rows, :], ws_hi[:, source]).astype(BF16)
                wn_lo[rows, block] = dot(gt[rows, :], ws_lo[:, source]).astype(BF16)

            tiles(leaf, leaf_tile, body)
        return swap

    def half_m():
        return pl.ds(pl.multiple_of(place.core * (rank // 2), rank // 2), rank // 2)

    def corrections_pass(swap):
        swap.wait_recv()
        ref = m_in.at[half_m()]
        return send(ref, ref, once, 6, place.twin)

    def corrections(swap):
        swap.wait_recv()
        one, two = pl.ds(0, rank), pl.ds(rank, rank)
        k_hi[:, one], k_lo[:, one] = halves(m_out[:, one] + m_in[:, two])
        k_hi[:, two], k_lo[:, two] = halves(m_out[:, two] + m_in[:, one])

    one, two = pl.ds(0, rank), pl.ds(rank, rank)
    state_columns = pl.ds(0, leaf)

    def correct(rows, i, at, size):
        block = pl.ds(at * rank, size * rank)
        nat[rows, lane(i)] -= dot_beside(wn_hi[rows, block], wn_lo[rows, block], c_hl[block, :])

    def first(i, more=None):
        if more is not None:
            more.wait_recv()
        z = None
        for k, rows in enumerate(row_parts):
            sum_swaps[i][k].wait_recv()
            whole = x[rows, lane(i)] + y_in[i, rows, :]
            x_hl[rows, :] = beside(whole if more is None else whole + u_in[rows, :])
            term = dot_beside(b_hi[:, rows], b_lo[:, rows], x_hl[rows, :])
            z = term if z is None else z + term
        z_out[i] = z
        if i == direct:
            own = beside(z_out[i, one, :])
            z_out[i, two, :] = z_out[i, two, :] - dot_beside(k_hi[:, two], k_lo[:, two], own)
            far_swaps.append(send(z_out.at[i, two], far_in, once, 7, place.far))
            t_swaps[i] = send(z_out.at[i, two], t_in.at[i], per, (3, i), place.cross)
        z_swaps[i] = send(z_out.at[i], z_in.at[i], per, (2, i), place.mate)

        def state(rows):
            st_hl[rows, :] = beside(dot_beside(ws_hi[rows, state_columns], ws_lo[rows, state_columns], x_hl[...]))

        tiles(leaf, leaf_tile, state)

        def natural(rows):
            nat[rows, lane(i)] = fold(dot(gt[rows, :], st_hl[...]))

        tiles(leaf, leaf_tile, natural)

    def second(i):
        z_swaps[i].wait_recv()
        c_hl[one, :] = beside(z_in[i, one, :])
        c_hl[two, :] = beside(z_out[i, one, :])
        both = pl.ds(0, 2 * rank)
        total = z_out[i, two, :] + z_in[i, two, :] - dot_beside(k_hi[...], k_lo[...], c_hl[both, :])
        t_out[i] = total
        t_swaps[i] = send(t_out.at[i], t_in.at[i], per, (3, i), place.cross)
        c_hl[pl.ds(3 * rank, rank), :] = beside(total)

        def update(rows):
            correct(rows, i, 0, 2)
            correct(rows, i, 3, 1)

        tiles(leaf, leaf_tile, update)

    def third(i):
        t_swaps[i].wait_recv()
        c_hl[pl.ds(2 * rank, rank), :] = beside(t_in[i])
        tiles(leaf, leaf_tile, lambda rows: correct(rows, i, 2, 1))

    def at_once(i):
        z_swaps[i].wait_recv()
        c_hl[one, :] = beside(z_in[i, one, :])
        c_hl[two, :] = beside(z_out[i, one, :])
        c_hl[pl.ds(3 * rank, rank), :] = beside(z_out[i, two, :] + z_in[i, two, :])
        t_swaps[i].wait_recv()
        far_swaps[0].wait_recv()
        c_hl[pl.ds(2 * rank, rank), :] = beside(t_in[i] + far_in[...])
        tiles(leaf, leaf_tile, lambda rows: correct(rows, i, 0, 4))

    direct = last - 1
    far_swaps = []
    near_chunk(0)
    own_sums(1)
    wt_g.ring2_pass(0)
    wt_g.ring2_pass(3)
    near_chunk(1)
    wt_g.ring2_pass(1)
    wt_g.ring2_pass(2)
    own_sums(last)
    mate_sums = pass_on()
    wt_g.to_twin(3)
    wt_g.to_twin(1)
    for i in range(2, last):
        own_sums(i)
        near_chunk(i)
    for off1 in (0, 3, 1, 2):
        wt_g.end_to_twin(off1)
    wt_g.from_twin()
    m_swap = weights()
    first(0)
    first(last, mate_sums)
    m_swap = corrections_pass(m_swap)
    first(1)
    corrections(m_swap)
    for i in (0, last, 1):
        second(i)
    first(direct)
    for i in (0, last, 1):
        third(i)
    final = [far_swaps[0], t_swaps[direct], z_swaps[direct]]
    for copy in started:
        if not any(copy is other for other in final):
            copy.wait_send()
    for g in (*near_gs, wt_g):
        g.finish()
    at_once(direct)
    for copy in final:
        copy.wait_send()


def per_device(
    incident, sources, tree_order, near_quad, near_owner, near_slot, leaf_inverse, basis_v, basis_w
):
    leaf, cols = incident.shape
    near = near_quad.shape[0]
    rank = basis_v.shape[2]
    group = lax.axis_size("col")
    rows = leaf // group
    chunks = cols // LANES
    width = leaf + 6 * rank
    vmem, sem = pltpu.VMEM, pltpu.SemaphoreType.DMA

    def f32(*shape):
        return vmem(shape, F32)

    def pair(*shape):
        return [vmem(shape, BF16), vmem(shape, BF16)]

    scratch = [
        vmem((1, leaf), jnp.int32), vmem((1, near), jnp.int32), vmem((1, near), jnp.int32),
        f32(rows, leaf), f32(2, rows, rank), f32(2, 2, rows, rank),
        f32(near, leaf), f32(leaf, cols), f32(leaf, cols),
        f32(2, group, near // (2 * group), leaf), f32(group, rows, width),
        vmem((1, near), jnp.int32), vmem((1, near), jnp.int32),
        f32(chunks, leaf, LANES), f32(chunks, leaf, LANES), f32(chunks, leaf, LANES),
        f32(chunks, 2 * rank, LANES), f32(chunks, 2 * rank, LANES),
        f32(chunks, rank, LANES), f32(chunks, rank, LANES),
        f32(leaf, LANES), f32(leaf, LANES), f32(leaf, LANES), f32(leaf, LANES),
        f32(rank, 2 * rank), f32(rank, 2 * rank), f32(rank, LANES),
        *pair(near, leaf), vmem((chunks, leaf, 2 * LANES), BF16), vmem((chunks, near, 2 * LANES), BF16),
        vmem((6, leaf, near), BF16), vmem((leaf, leaf), BF16),
        *pair(2 * rank, leaf), *pair(2 * rank, leaf),
        *pair(leaf, leaf + 4 * rank), *pair(leaf, 4 * rank),
        *pair(rank, 2 * rank), vmem((leaf, 2 * LANES), BF16), vmem((4 * rank, 2 * LANES), BF16),
        vmem((leaf, 2 * LANES), BF16), f32(leaf, 2 * rank),
        sem((3, 32)), sem((3, 32)), sem((5, chunks)), sem((5, chunks)), sem((8,)), sem((8,)),
        sem((9,)),
    ]
    in_any = pl.BlockSpec(memory_space=pl.ANY)
    return pl.pallas_call(
        kernel,
        out_shape=pltpu.VMEM((leaf, cols), F32),
        in_specs=[in_any] * 9,
        out_specs=pl.BlockSpec(memory_space=pltpu.VMEM),
        scratch_shapes=scratch,
        compiler_params=pltpu.CompilerParams(
            collective_id=0, has_side_effects=True, vmem_limit_bytes=54 * 1024 * 1024
        ),
        cost_estimate=pl.CostEstimate(flops=15 * 10**9, bytes_accessed=12 * 10**6, transcendentals=0),
    )(
        tree_order, near_owner.reshape(1, near), near_slot.reshape(1, near),
        leaf_inverse, basis_v, basis_w, incident, sources, near_quad,
    )

def solution(mesh):
    placed = (
        P("leaf", "col"),
        P("leaf", "col"),
        P("leaf", None),
        P("leaf", None),
        P("leaf", None),
        P("leaf"),
        P(("leaf", "col"), None),
        P(None, ("leaf", "col"), None),
        P(None, None, ("leaf", "col"), None),
    )
    return jax.shard_map(
        per_device, mesh=mesh, in_specs=placed, out_specs=P("leaf", "col"), check_vma=False
    )
```

```python
import functools
import math

import jax
import jax.numpy as jnp
from jax import lax
from jax.experimental import pallas as pl
from jax.experimental.pallas import tpu as pltpu
from jax.sharding import PartitionSpec as P

MESH = pl.DeviceIdType.MESH
F32 = jnp.float32
BF16 = jnp.bfloat16
LANES = 128
RING = 4


def halves(value):
    top = value.astype(BF16)
    return top, (value - top.astype(F32)).astype(BF16)


def dot(a, b):
    return jnp.dot(a, b, preferred_element_type=F32)


def dot3(a_hi, a_lo, b_hi, b_lo):
    return dot(a_hi, b_hi) + dot(a_hi, b_lo) + dot(a_lo, b_hi)


def beside(value):
    return jnp.concatenate(halves(value), axis=1)


def fold(wide):
    return wide[:, :LANES] + wide[:, LANES:]


def dot_beside(a_hi, a_lo, b):
    return fold(dot(a_hi, b)) + dot(a_lo, b[:, :LANES])


def tiles(count, size, body):
    def step(index, carry):
        body(pl.ds(pl.multiple_of(index * size, size), size))
        return carry

    lax.fori_loop(0, count // size, step, 0)


class Place:
    def __init__(self):
        self.leaf = lax.axis_index("leaf")
        self.col = lax.axis_index("col")
        self.core = self.col % 2
        y = (self.col // 2) % RING
        z = self.col // (2 * RING)
        self.d1 = y * (1 - self.core) + z * self.core
        self.d2 = z * (1 - self.core) + y * self.core
        self.twin = (self.leaf, self.col + 1 - 2 * self.core)
        self.mate = (self.leaf + 1 - 2 * (self.leaf % 2), self.col)
        self.cross = (3 - self.leaf, self.col)
        self.right1 = self.device(0, 1)
        self.left1 = self.device(0, RING - 1)
        self.opposite1 = self.device(0, 2)
        self.far = (self.leaf + 2 - 4 * (self.leaf // 2), self.col)
        self.right2 = self.device(1, 0)
        self.left2 = self.device(RING - 1, 0)

    def device(self, off2, off1):
        a, b, core = (self.d2 + off2) % RING, (self.d1 + off1) % RING, self.core
        return self.leaf, (a * 2 * RING + b * 2) * (1 - core) + (b * 2 * RING + a * 2 + 1) * core

    def group(self, off2):
        return (self.core * RING + (self.d2 + off2) % RING) * RING

    def twin_group(self, off2):
        return ((1 - self.core) * RING + (self.d1 + off2) % RING) * RING

    def index(self, off2, off1):
        return self.group(off2) + (self.d1 + off1) % RING

    def twin_index(self, off2, off1):
        return self.twin_group(off2) + (self.d2 + off1) % RING


class Gather:
    def __init__(self, place, buf, send_sem, recv_sem):
        self.p, self.buf, self.ss, self.rs = place, buf, send_sem, recv_sem
        self.started = []

    def piece(self, off2, off1):
        return self.buf.at[self.p.index(off2, off1)]

    def send(self, ref, sem, device):
        copy = pltpu.make_async_remote_copy(
            src_ref=ref, dst_ref=ref, send_sem=self.ss.at[sem], recv_sem=self.rs.at[sem],
            device_id=device, device_id_type=MESH,
        )
        copy.start()
        self.started.append(copy)

    def recv(self, ref, sem):
        pltpu.make_async_remote_copy(
            src_ref=ref, dst_ref=ref, send_sem=self.ss.at[sem], recv_sem=self.rs.at[sem],
            device_id=self.p.twin, device_id_type=MESH,
        ).wait_recv()

    def ring1(self):
        own = self.piece(0, 0)
        self.send(own, 0, self.p.right1)
        self.send(own, 1, self.p.left1)
        self.send(own, 2, self.p.opposite1)

    def ring1_recv(self, off1):
        self.recv(self.piece(0, off1), (3, 1, 2).index(off1))

    def ring2(self, off1):
        self.send(self.piece(0, off1), 4 + off1, self.p.right2)
        self.send(self.piece(0, off1), 8 + off1, self.p.left2)

    def ring2_pass(self, off1):
        self.recv(self.piece(3, off1), 4 + off1)
        if off1 in (0, 1):
            self.send(self.piece(3, off1), 12 + off1, self.p.right2)
        self.recv(self.piece(1, off1), 8 + off1)
        if off1 in (3, 2):
            self.send(self.piece(1, off1), 12 + off1, self.p.left2)

    def ring2_end(self, off1):
        self.recv(self.piece(2, off1), 12 + off1)

    def to_twin(self, off2):
        self.send(self.buf.at[pl.ds(self.p.group(off2), RING)], 16 + off2, self.p.twin)

    def end_to_twin(self, off1):
        self.ring2_end(off1)
        self.send(self.piece(2, off1), 20 + off1, self.p.twin)

    def from_twin(self):
        for off2 in (0, 3, 1):
            self.recv(self.buf.at[pl.ds(self.p.twin_group(off2), RING)], 16 + off2)
        for off1 in (0, 3, 1, 2):
            self.recv(self.buf.at[self.p.twin_index(2, off1)], 20 + off1)

    def finish(self):
        for copy in self.started:
            copy.wait_send()


def kernel(
    tree_any, owner_any, slot_any, inverse_any, basis_v_any, basis_w_any, incident, sources, near_quad, nat,
    tree, owner, slot, inverse, basis_v, basis_w,
    nq, s_own, x, nqp, wt, key_out, key_in, s_in, y_out, y_in, z_out, z_in, t_out, t_in, u_out, u_in, w_out, w_in,
    m_out, m_in, far_in,
    nq_hi, nq_lo, s_hl, p_hl, oh, gt, vt_hi, vt_lo, b_hi, b_lo, ws_hi, ws_lo, wn_hi, wn_lo,
    k_hi, k_lo, x_hl, c_hl, st_hl, v_all,
    gsend, grecv, csend, crecv, osend, orecv, load_sem,
):
    leaf, cols = incident.shape
    near = near_quad.shape[0]
    rank = basis_v.shape[2]
    part = nqp.shape[2]
    group = nqp.shape[1]
    chunks = cols // LANES
    last = chunks - 1
    near_tile, leaf_tile = near // 2, leaf // 2
    row_parts = (pl.ds(0, 2 * leaf // 3), pl.ds(2 * leaf // 3, leaf // 3))
    place = Place()
    mine = place.index(0, 0)
    started = []

    def lane(i):
        return pl.ds(i * LANES, LANES)

    pairs = (
        (tree_any, tree), (owner_any, owner), (slot_any, slot), (inverse_any, inverse), (basis_v_any, basis_v),
        (basis_w_any, basis_w), (near_quad, nq), (sources, s_own), (incident, x),
    )
    loads = [pltpu.make_async_copy(src, dst, load_sem.at[i]) for i, (src, dst) in enumerate(pairs)]
    barrier = pltpu.get_barrier_semaphore()
    neighbours = (
        place.mate, place.cross, place.far, place.twin, place.right1, place.left1, place.opposite1, place.right2,
        place.left2,
    )
    for device in neighbours:
        pl.semaphore_signal(barrier, inc=1, device_id=device, device_id_type=MESH)
    for copy in loads:
        copy.start()

    def send(src, dst, sems, index, device):
        copy = pltpu.make_async_remote_copy(
            src_ref=src, dst_ref=dst, send_sem=sems[0].at[index], recv_sem=sems[1].at[index],
            device_id=device, device_id_type=MESH,
        )
        copy.start()
        started.append(copy)
        return copy

    near_gs = [Gather(place, nqp.at[h], gsend.at[h], grecv.at[h]) for h in range(2)]
    wt_g = Gather(place, wt, gsend.at[2], grecv.at[2])

    def make_gt(rows):
        number = rows.start + lax.broadcasted_iota(jnp.int32, (rows.size, leaf), 0)
        gt[rows, :] = jnp.where(number == tree[...], 1.0, 0.0).astype(BF16)

    def make_one_hot(which, key, block):
        base = block * leaf

        def body(rows):
            number = base + rows.start + lax.broadcasted_iota(jnp.int32, (rows.size, near), 0)
            oh[which, rows, :] = jnp.where(number == key[0:1, :], 1.0, 0.0).astype(BF16)

        tiles(leaf, LANES, body)

    def split_near(rows):
        nq_hi[rows, :], nq_lo[rows, :] = halves(nq[rows, :])

    def partial_rows(i, rows):
        p_hl[i, rows, :] = beside(dot_beside(nq_hi[rows, :], nq_lo[rows, :], s_hl[i]))

    def partial(i):
        tiles(near, near_tile, lambda rows: partial_rows(i, rows))

    def own_partial(i):
        def body(rows):
            s_hl[i, rows, :] = beside(s_own[rows, lane(i)])

        tiles(leaf, LANES, body)
        partial(i)

    def sums(which, i, rows):
        return fold(dot(oh[which, rows, :], p_hl[i]))

    for copy in loads[:6]:
        copy.wait()
    key_out[...] = owner[...] * leaf + slot[...]
    tiles(leaf, LANES, make_gt)
    nt = (((1,), (1,)), ((), ()))
    top, low = halves(inverse[...])
    wt[mine, :, pl.ds(0, leaf)] = lax.dot_general(
        top, gt[...], nt, preferred_element_type=F32
    ) + lax.dot_general(low, gt[...], nt, preferred_element_type=F32)
    for k in range(4):
        wt[mine, :, pl.ds(leaf + k * rank, rank)] = basis_w[k // 2, k % 2]
    for k in range(2):
        wt[mine, :, pl.ds(leaf + (4 + k) * rank, rank)] = basis_v[k]
    make_one_hot(1, key_out, place.cross[0])
    make_one_hot(3, key_out, place.far[0])
    loads[6].wait()
    tiles(near, LANES, split_near)

    pl.semaphore_wait(barrier, len(neighbours))

    once, per = (osend, orecv), (csend, crecv)
    near_swaps = [
        send(
            near_quad.at[pl.ds(pl.multiple_of(h * near // 2 + mine * part, part), part)], nqp.at[h, mine],
            once, h, place.mate,
        )
        for h in range(2)
    ]
    key_swap = send(key_out, key_in, once, 2, place.mate)
    wt_g.ring1()
    source_swaps = [
        send(sources.at[:, lane(i)], s_in.at[i], per, (0, i), place.mate) for i in range(last)
    ]

    def send_sums(i, part):
        rows = row_parts[part]
        return send(y_out.at[i, rows], y_in.at[i, rows], per, (1 + 3 * part, i), place.cross)

    loads[7].wait()
    own_partial(last)
    sum_swaps = {last: []}
    for k in range(2):
        y_out[last, row_parts[k], :] = sums(1, last, row_parts[k])
        sum_swaps[last].append(send_sums(last, k))

    def last_far(rows):
        w_out[rows, :] = sums(3, last, rows)

    tiles(leaf, leaf_tile, last_far)
    far_swap = send(w_out, w_in, once, 3, place.cross)
    make_one_hot(0, key_out, place.leaf)
    make_one_hot(2, key_out, place.mate[0])
    loads[8].wait()

    def own_sums(i):
        def body(rows):
            x[rows, lane(i)] += sums(0, i, rows)
            if i < last:
                y_out[i, rows, :] = sums(1, i, rows)
            else:
                u_out[rows, :] = sums(2, i, rows)

        tiles(leaf, leaf_tile, body)

    def split_swapped(i):
        source_swaps[i].wait_recv()

        def body(rows):
            s_hl[i, rows, :] = beside(s_in[i, rows, :])

        tiles(leaf, LANES, body)

    for g, swap in zip(near_gs, near_swaps):
        swap.wait_recv()
        g.ring1()
        g.ring2(0)
    own_partial(0)
    own_sums(0)
    for g in near_gs:
        for off1 in (3, 1, 2):
            g.ring1_recv(off1)
            g.ring2(off1)
        g.ring2_pass(0)
    for g in near_gs:
        g.to_twin(0)
    own_partial(1)
    for g in near_gs:
        for off1 in (3, 1, 2):
            g.ring2_pass(off1)
    wt_g.ring2(0)
    for off1 in (3, 1, 2):
        wt_g.ring1_recv(off1)
        wt_g.ring2(off1)
    for g in near_gs:
        g.to_twin(3)
        g.to_twin(1)
    key_swap.wait_recv()
    make_one_hot(5, key_in, place.cross[0])
    split_swapped(0)
    for off1 in (0, 3, 1, 2):
        near_gs[0].end_to_twin(off1)
    for i in range(2, last):
        own_partial(i)
    for off1 in (0, 3, 1, 2):
        near_gs[1].end_to_twin(off1)
    wt_g.to_twin(0)

    def split_partner(h):
        count = 4 * part

        def body(index, carry):
            rows = pl.ds(pl.multiple_of(h * near // 2 + index * count, count), count)
            block = nqp[h, pl.ds(4 * index, 4)].reshape(count, leaf)
            nq_hi[rows, :], nq_lo[rows, :] = halves(block)
            return carry

        lax.fori_loop(0, group // 4, body, 0)

    z_swaps, t_swaps = {}, {}

    def near_chunk(i):
        if i > 0:
            split_swapped(i)
        if i == 0:
            span = [pl.ds(h * near // 2, near // 2) for h in range(2)]
            for h in range(2):
                near_gs[h].from_twin()
                split_partner(h)
                partial_rows(i, span[h])
                if h == 0:
                    for rows in row_parts:
                        y_out[i, rows, :] += fold(dot(oh[5, rows, span[0]], p_hl[i, span[0], :]))
        else:
            partial(i)
        sum_swaps[i] = []
        for k, rows in enumerate(row_parts):
            if i == 0:
                y_out[i, rows, :] += fold(dot(oh[5, rows, span[1]], p_hl[i, span[1], :]))
            else:
                y_out[i, rows, :] += sums(5, i, rows)
            sum_swaps[i].append(send_sums(i, k))
        if i == 0:
            make_one_hot(4, key_in, place.leaf)

        def here(rows):
            x[rows, lane(i)] += sums(4, i, rows)

        tiles(leaf, leaf_tile, here)

    def pass_on():
        far_swap.wait_recv()

        def body(rows):
            u_out[rows, :] += w_in[rows, :]

        tiles(leaf, LANES, body)
        return send(u_out, u_in, once, 4, place.mate)

    def weights():
        count = inverse.shape[0]
        scale = [1.0 / math.sqrt(2**k * leaf) for k in range(2)]

        def split(pair, carry):
            rows = pl.ds(pl.multiple_of(pair * 2 * count, 16), 2 * count)
            other = RING * RING + (pair % RING) * RING + pair // RING
            both = jnp.concatenate([wt[pair], wt[other]], axis=0)
            ws_hi[rows, :], ws_lo[rows, :] = halves(both[:, : leaf + 4 * rank])
            for k in range(2):
                at = leaf + (4 + k) * rank
                v_all[rows, pl.ds(k * rank, rank)] = both[:, at : at + rank] * scale[k]
            return carry

        lax.fori_loop(0, RING * RING, split, 0)
        vt_hi[...], vt_lo[...] = halves(v_all[...].T)
        second_v = pl.ds(rank, rank)
        first_w = pl.ds(leaf, 2 * rank)
        m_out[...] = dot3(vt_hi[second_v, :], vt_lo[second_v, :], ws_hi[:, first_w], ws_lo[:, first_w])
        mine_m = half_m()
        swap = send(m_out.at[mine_m], m_in.at[mine_m], once, 5, place.mate)
        step = min(256, leaf)
        for k in range(leaf // step):
            block = pl.ds(k * step, step)
            r = dot3(vt_hi[...], vt_lo[...], ws_hi[:, block], ws_lo[:, block])
            b_hi[:, block], b_lo[:, block] = halves(r)
        for k in range(2):
            block, source = pl.ds(2 * k * rank, 2 * rank), pl.ds(leaf + 2 * k * rank, 2 * rank)

            def body(rows):
                wn_hi[rows, block] = dot(gt[rows, :], ws_hi[:, source]).astype(BF16)
                wn_lo[rows, block] = dot(gt[rows, :], ws_lo[:, source]).astype(BF16)

            tiles(leaf, leaf_tile, body)
        return swap

    def half_m():
        return pl.ds(pl.multiple_of(place.core * (rank // 2), rank // 2), rank // 2)

    def corrections_pass(swap):
        swap.wait_recv()
        ref = m_in.at[half_m()]
        return send(ref, ref, once, 6, place.twin)

    def corrections(swap):
        swap.wait_recv()
        one, two = pl.ds(0, rank), pl.ds(rank, rank)
        k_hi[:, one], k_lo[:, one] = halves(m_out[:, one] + m_in[:, two])
        k_hi[:, two], k_lo[:, two] = halves(m_out[:, two] + m_in[:, one])

    one, two = pl.ds(0, rank), pl.ds(rank, rank)
    state_columns = pl.ds(0, leaf)

    def correct(rows, i, at, size):
        block = pl.ds(at * rank, size * rank)
        nat[rows, lane(i)] -= dot_beside(wn_hi[rows, block], wn_lo[rows, block], c_hl[block, :])

    def first(i, more=None):
        if more is not None:
            more.wait_recv()
        z = None
        for k, rows in enumerate(row_parts):
            sum_swaps[i][k].wait_recv()
            whole = x[rows, lane(i)] + y_in[i, rows, :]
            x_hl[rows, :] = beside(whole if more is None else whole + u_in[rows, :])
            term = dot_beside(b_hi[:, rows], b_lo[:, rows], x_hl[rows, :])
            z = term if z is None else z + term
        z_out[i] = z
        if i == direct:
            own = beside(z_out[i, one, :])
            z_out[i, two, :] = z_out[i, two, :] - dot_beside(k_hi[:, two], k_lo[:, two], own)
            far_swaps.append(send(z_out.at[i, two], far_in, once, 7, place.far))
            t_swaps[i] = send(z_out.at[i, two], t_in.at[i], per, (3, i), place.cross)
        z_swaps[i] = send(z_out.at[i], z_in.at[i], per, (2, i), place.mate)

        def state(rows):
            st_hl[rows, :] = beside(dot_beside(ws_hi[rows, state_columns], ws_lo[rows, state_columns], x_hl[...]))

        tiles(leaf, leaf_tile, state)

        def natural(rows):
            nat[rows, lane(i)] = fold(dot(gt[rows, :], st_hl[...]))

        tiles(leaf, leaf_tile, natural)

    def second(i):
        z_swaps[i].wait_recv()
        c_hl[one, :] = beside(z_in[i, one, :])
        c_hl[two, :] = beside(z_out[i, one, :])
        both = pl.ds(0, 2 * rank)
        total = z_out[i, two, :] + z_in[i, two, :] - dot_beside(k_hi[...], k_lo[...], c_hl[both, :])
        t_out[i] = total
        t_swaps[i] = send(t_out.at[i], t_in.at[i], per, (3, i), place.cross)
        c_hl[pl.ds(3 * rank, rank), :] = beside(total)

        def update(rows):
            correct(rows, i, 0, 2)
            correct(rows, i, 3, 1)

        tiles(leaf, leaf_tile, update)

    def third(i):
        t_swaps[i].wait_recv()
        c_hl[pl.ds(2 * rank, rank), :] = beside(t_in[i])
        tiles(leaf, leaf_tile, lambda rows: correct(rows, i, 2, 1))

    def at_once(i):
        z_swaps[i].wait_recv()
        c_hl[one, :] = beside(z_in[i, one, :])
        c_hl[two, :] = beside(z_out[i, one, :])
        c_hl[pl.ds(3 * rank, rank), :] = beside(z_out[i, two, :] + z_in[i, two, :])
        t_swaps[i].wait_recv()
        far_swaps[0].wait_recv()
        c_hl[pl.ds(2 * rank, rank), :] = beside(t_in[i] + far_in[...])
        tiles(leaf, leaf_tile, lambda rows: correct(rows, i, 0, 4))

    direct = last - 1
    far_swaps = []
    near_chunk(0)
    own_sums(1)
    wt_g.ring2_pass(0)
    wt_g.ring2_pass(3)
    near_chunk(1)
    wt_g.ring2_pass(1)
    wt_g.ring2_pass(2)
    own_sums(last)
    mate_sums = pass_on()
    wt_g.to_twin(3)
    wt_g.to_twin(1)
    for i in range(2, last):
        own_sums(i)
        near_chunk(i)
    for off1 in (0, 3, 1, 2):
        wt_g.end_to_twin(off1)
    wt_g.from_twin()
    m_swap = weights()
    first(0)
    first(last, mate_sums)
    m_swap = corrections_pass(m_swap)
    first(1)
    corrections(m_swap)
    for i in (0, last, 1):
        second(i)
    first(direct)
    for i in (0, last, 1):
        third(i)
    final = [far_swaps[0], t_swaps[direct], z_swaps[direct]]
    for copy in started:
        if not any(copy is other for other in final):
            copy.wait_send()
    for g in (*near_gs, wt_g):
        g.finish()
    at_once(direct)
    for copy in final:
        copy.wait_send()


def per_device(
    incident, sources, tree_order, near_quad, near_owner, near_slot, leaf_inverse, basis_v, basis_w
):
    leaf, cols = incident.shape
    near = near_quad.shape[0]
    rank = basis_v.shape[2]
    group = lax.axis_size("col")
    rows = leaf // group
    chunks = cols // LANES
    width = leaf + 6 * rank
    vmem, sem = pltpu.VMEM, pltpu.SemaphoreType.DMA

    def f32(*shape):
        return vmem(shape, F32)

    def pair(*shape):
        return [vmem(shape, BF16), vmem(shape, BF16)]

    scratch = [
        vmem((1, leaf), jnp.int32), vmem((1, near), jnp.int32), vmem((1, near), jnp.int32),
        f32(rows, leaf), f32(2, rows, rank), f32(2, 2, rows, rank),
        f32(near, leaf), f32(leaf, cols), f32(leaf, cols),
        f32(2, group, near // (2 * group), leaf), f32(group, rows, width),
        vmem((1, near), jnp.int32), vmem((1, near), jnp.int32),
        f32(chunks, leaf, LANES), f32(chunks, leaf, LANES), f32(chunks, leaf, LANES),
        f32(chunks, 2 * rank, LANES), f32(chunks, 2 * rank, LANES),
        f32(chunks, rank, LANES), f32(chunks, rank, LANES),
        f32(leaf, LANES), f32(leaf, LANES), f32(leaf, LANES), f32(leaf, LANES),
        f32(rank, 2 * rank), f32(rank, 2 * rank), f32(rank, LANES),
        *pair(near, leaf), vmem((chunks, leaf, 2 * LANES), BF16), vmem((chunks, near, 2 * LANES), BF16),
        vmem((6, leaf, near), BF16), vmem((leaf, leaf), BF16),
        *pair(2 * rank, leaf), *pair(2 * rank, leaf),
        *pair(leaf, leaf + 4 * rank), *pair(leaf, 4 * rank),
        *pair(rank, 2 * rank), vmem((leaf, 2 * LANES), BF16), vmem((4 * rank, 2 * LANES), BF16),
        vmem((leaf, 2 * LANES), BF16), f32(leaf, 2 * rank),
        sem((3, 32)), sem((3, 32)), sem((5, chunks)), sem((5, chunks)), sem((8,)), sem((8,)),
        sem((9,)),
    ]
    in_any = pl.BlockSpec(memory_space=pl.ANY)
    return pl.pallas_call(
        kernel,
        out_shape=pltpu.VMEM((leaf, cols), F32),
        in_specs=[in_any] * 9,
        out_specs=pl.BlockSpec(memory_space=pltpu.VMEM),
        scratch_shapes=scratch,
        compiler_params=pltpu.CompilerParams(
            collective_id=0, has_side_effects=True, vmem_limit_bytes=54 * 1024 * 1024
        ),
        cost_estimate=pl.CostEstimate(flops=15 * 10**9, bytes_accessed=12 * 10**6, transcendentals=0),
    )(
        tree_order, near_owner.reshape(1, near), near_slot.reshape(1, near),
        leaf_inverse, basis_v, basis_w, incident, sources, near_quad,
    )

def solution(mesh):
    placed = (
        P("leaf", "col"),
        P("leaf", "col"),
        P("leaf", None),
        P("leaf", None),
        P("leaf", None),
        P("leaf"),
        P(("leaf", "col"), None),
        P(None, ("leaf", "col"), None),
        P(None, None, ("leaf", "col"), None),
    )
    return jax.shard_map(
        per_device, mesh=mesh, in_specs=placed, out_specs=P("leaf", "col"), check_vma=False
    )
```

```python
import functools
import math

import jax
import jax.numpy as jnp
from jax import lax
from jax.experimental import pallas as pl
from jax.experimental.pallas import tpu as pltpu
from jax.sharding import PartitionSpec as P

MESH = pl.DeviceIdType.MESH
F32 = jnp.float32
BF16 = jnp.bfloat16
LANES = 128
RING = 4


def halves(value):
    top = value.astype(BF16)
    return top, (value - top.astype(F32)).astype(BF16)


def dot(a, b):
    return jnp.dot(a, b, preferred_element_type=F32)


def dot3(a_hi, a_lo, b_hi, b_lo):
    return dot(a_hi, b_hi) + dot(a_hi, b_lo) + dot(a_lo, b_hi)


def beside(value):
    return jnp.concatenate(halves(value), axis=1)


def fold(wide):
    return wide[:, :LANES] + wide[:, LANES:]


def dot_beside(a_hi, a_lo, b):
    return fold(dot(a_hi, b)) + dot(a_lo, b[:, :LANES])


def tiles(count, size, body):
    def step(index, carry):
        body(pl.ds(pl.multiple_of(index * size, size), size))
        return carry

    lax.fori_loop(0, count // size, step, 0)


class Place:
    def __init__(self):
        self.leaf = lax.axis_index("leaf")
        self.col = lax.axis_index("col")
        self.core = self.col % 2
        y = (self.col // 2) % RING
        z = self.col // (2 * RING)
        self.d1 = y * (1 - self.core) + z * self.core
        self.d2 = z * (1 - self.core) + y * self.core
        self.twin = (self.leaf, self.col + 1 - 2 * self.core)
        self.mate = (self.leaf + 1 - 2 * (self.leaf % 2), self.col)
        self.cross = (3 - self.leaf, self.col)
        self.right1 = self.device(0, 1)
        self.left1 = self.device(0, RING - 1)
        self.opposite1 = self.device(0, 2)
        self.far = (self.leaf + 2 - 4 * (self.leaf // 2), self.col)
        self.right2 = self.device(1, 0)
        self.left2 = self.device(RING - 1, 0)

    def device(self, off2, off1):
        a, b, core = (self.d2 + off2) % RING, (self.d1 + off1) % RING, self.core
        return self.leaf, (a * 2 * RING + b * 2) * (1 - core) + (b * 2 * RING + a * 2 + 1) * core

    def group(self, off2):
        return (self.core * RING + (self.d2 + off2) % RING) * RING

    def twin_group(self, off2):
        return ((1 - self.core) * RING + (self.d1 + off2) % RING) * RING

    def index(self, off2, off1):
        return self.group(off2) + (self.d1 + off1) % RING

    def twin_index(self, off2, off1):
        return self.twin_group(off2) + (self.d2 + off1) % RING


class Gather:
    def __init__(self, place, buf, send_sem, recv_sem):
        self.p, self.buf, self.ss, self.rs = place, buf, send_sem, recv_sem
        self.started = []

    def piece(self, off2, off1):
        return self.buf.at[self.p.index(off2, off1)]

    def send(self, ref, sem, device):
        copy = pltpu.make_async_remote_copy(
            src_ref=ref, dst_ref=ref, send_sem=self.ss.at[sem], recv_sem=self.rs.at[sem],
            device_id=device, device_id_type=MESH,
        )
        copy.start()
        self.started.append(copy)

    def recv(self, ref, sem):
        pltpu.make_async_remote_copy(
            src_ref=ref, dst_ref=ref, send_sem=self.ss.at[sem], recv_sem=self.rs.at[sem],
            device_id=self.p.twin, device_id_type=MESH,
        ).wait_recv()

    def ring1(self):
        own = self.piece(0, 0)
        self.send(own, 0, self.p.right1)
        self.send(own, 1, self.p.left1)
        self.send(own, 2, self.p.opposite1)

    def ring1_recv(self, off1):
        self.recv(self.piece(0, off1), (3, 1, 2).index(off1))

    def ring2(self, off1):
        self.send(self.piece(0, off1), 4 + off1, self.p.right2)
        self.send(self.piece(0, off1), 8 + off1, self.p.left2)

    def ring2_pass(self, off1):
        self.recv(self.piece(3, off1), 4 + off1)
        if off1 in (0, 1):
            self.send(self.piece(3, off1), 12 + off1, self.p.right2)
        self.recv(self.piece(1, off1), 8 + off1)
        if off1 in (3, 2):
            self.send(self.piece(1, off1), 12 + off1, self.p.left2)

    def ring2_end(self, off1):
        self.recv(self.piece(2, off1), 12 + off1)

    def to_twin(self, off2):
        self.send(self.buf.at[pl.ds(self.p.group(off2), RING)], 16 + off2, self.p.twin)

    def end_to_twin(self, off1):
        self.ring2_end(off1)
        self.send(self.piece(2, off1), 20 + off1, self.p.twin)

    def from_twin(self):
        for off2 in (0, 3, 1):
            self.recv(self.buf.at[pl.ds(self.p.twin_group(off2), RING)], 16 + off2)
        for off1 in (0, 3, 1, 2):
            self.recv(self.buf.at[self.p.twin_index(2, off1)], 20 + off1)

    def finish(self):
        for copy in self.started:
            copy.wait_send()


def kernel(
    tree_any, owner_any, slot_any, inverse_any, basis_v_any, basis_w_any, incident, sources, near_quad, nat,
    tree, owner, slot, inverse, basis_v, basis_w,
    nq, s_own, x, nqp_first, nqp_second, wt, key_out, key_in, s_in, y_out, y_in, z_out, z_in, t_out, t_in, u_out, u_in, w_out, w_in,
    m_out, m_in, far_in,
    nq_hi, nq_lo, s_hl, p_hl, oh, gt, vt_hi, vt_lo, b_hi, b_lo, ws_hi, ws_lo, wn_hi, wn_lo,
    k_hi, k_lo, x_hl, c_hl, st_hl, v_all,
    gsend, grecv, csend, crecv, osend, orecv, load_sem,
):
    leaf, cols = incident.shape
    near = near_quad.shape[0]
    rank = basis_v.shape[2]
    nqp = (nqp_first, nqp_second)
    group = nqp_first.shape[0]
    cut = group * nqp_first.shape[1]
    span = [pl.ds(0, cut), pl.ds(cut, near - cut)]
    chunks = cols // LANES
    last = chunks - 1
    near_tile, leaf_tile = near // 2, leaf // 2
    row_parts = (pl.ds(0, 2 * leaf // 3), pl.ds(2 * leaf // 3, leaf // 3))
    place = Place()
    mine = place.index(0, 0)
    started = []

    def lane(i):
        return pl.ds(i * LANES, LANES)

    others = pl.ds(0, last * LANES)
    pairs = (
        (tree_any, tree), (owner_any, owner), (slot_any, slot), (inverse_any, inverse), (basis_v_any, basis_v),
        (basis_w_any, basis_w), (near_quad, nq), (sources.at[:, lane(last)], s_own.at[:, lane(last)]), (incident, x),
        (sources.at[:, others], s_own.at[:, others]),
    )
    loads = [pltpu.make_async_copy(src, dst, load_sem.at[i]) for i, (src, dst) in enumerate(pairs)]
    barrier = pltpu.get_barrier_semaphore()
    neighbours = (
        place.mate, place.cross, place.far, place.twin, place.right1, place.left1, place.opposite1, place.right2,
        place.left2,
    )
    for device in neighbours:
        pl.semaphore_signal(barrier, inc=1, device_id=device, device_id_type=MESH)
    for copy in loads[:8]:
        copy.start()

    def send(src, dst, sems, index, device):
        copy = pltpu.make_async_remote_copy(
            src_ref=src, dst_ref=dst, send_sem=sems[0].at[index], recv_sem=sems[1].at[index],
            device_id=device, device_id_type=MESH,
        )
        copy.start()
        started.append(copy)
        return copy

    near_gs = [Gather(place, nqp[h], gsend.at[h], grecv.at[h]) for h in range(2)]
    wt_g = Gather(place, wt, gsend.at[2], grecv.at[2])

    def make_gt(rows):
        number = rows.start + lax.broadcasted_iota(jnp.int32, (rows.size, leaf), 0)
        gt[rows, :] = jnp.where(number == tree[...], 1.0, 0.0).astype(BF16)

    def make_one_hot(which, key, block):
        base = block * leaf

        def body(rows):
            number = base + rows.start + lax.broadcasted_iota(jnp.int32, (rows.size, near), 0)
            oh[which, rows, :] = jnp.where(number == key[0:1, :], 1.0, 0.0).astype(BF16)

        tiles(leaf, LANES, body)

    def split_near(rows):
        nq_hi[rows, :], nq_lo[rows, :] = halves(nq[rows, :])

    def partial_rows(i, rows):
        p_hl[i, rows, :] = beside(dot_beside(nq_hi[rows, :], nq_lo[rows, :], s_hl[i]))

    def partial(i):
        tiles(near, near_tile, lambda rows: partial_rows(i, rows))

    def own_partial(i):
        def body(rows):
            s_hl[i, rows, :] = beside(s_own[rows, lane(i)])

        tiles(leaf, LANES, body)
        partial(i)

    def sums(which, i, rows):
        return fold(dot(oh[which, rows, :], p_hl[i]))

    for copy in loads[:6]:
        copy.wait()
    key_out[...] = owner[...] * leaf + slot[...]
    tiles(leaf, LANES, make_gt)
    nt = (((1,), (1,)), ((), ()))
    top, low = halves(inverse[...])
    wt[mine, :, pl.ds(0, leaf)] = lax.dot_general(
        top, gt[...], nt, preferred_element_type=F32
    ) + lax.dot_general(low, gt[...], nt, preferred_element_type=F32)
    for k in range(4):
        wt[mine, :, pl.ds(leaf + k * rank, rank)] = basis_w[k // 2, k % 2]
    for k in range(2):
        wt[mine, :, pl.ds(leaf + (4 + k) * rank, rank)] = basis_v[k]

    pl.semaphore_wait(barrier, len(neighbours))

    once, per = (osend, orecv), (csend, crecv)
    near_swaps = [
        send(
            near_quad.at[pl.ds(pl.multiple_of(h * cut + mine * nqp[h].shape[1], 8), nqp[h].shape[1])],
            nqp[h].at[mine],
            once, h, place.mate,
        )
        for h in range(2)
    ]
    key_swap = send(key_out, key_in, once, 2, place.mate)
    wt_g.ring1()
    source_swaps = [
        send(sources.at[:, lane(i)], s_in.at[i], per, (0, i), place.mate) for i in range(last)
    ]

    def send_sums(i, part):
        rows = row_parts[part]
        return send(y_out.at[i, rows], y_in.at[i, rows], per, (1 + 3 * part, i), place.cross)

    for copy in loads[8:]:
        copy.start()
    loads[6].wait()
    tiles(near, LANES, split_near)
    loads[7].wait()
    own_partial(last)
    make_one_hot(1, key_out, place.cross[0])
    sum_swaps = {last: []}
    for k in range(2):
        y_out[last, row_parts[k], :] = sums(1, last, row_parts[k])
        sum_swaps[last].append(send_sums(last, k))

    make_one_hot(3, key_out, place.far[0])

    def last_far(rows):
        w_out[rows, :] = sums(3, last, rows)

    tiles(leaf, leaf_tile, last_far)
    far_swap = send(w_out, w_in, once, 3, place.cross)
    make_one_hot(0, key_out, place.leaf)
    make_one_hot(2, key_out, place.mate[0])
    loads[8].wait()
    loads[9].wait()

    def own_sums(i):
        def body(rows):
            x[rows, lane(i)] += sums(0, i, rows)
            if i < last:
                y_out[i, rows, :] = sums(1, i, rows)
            else:
                u_out[rows, :] = sums(2, i, rows)

        tiles(leaf, leaf_tile, body)

    def split_swapped(i):
        source_swaps[i].wait_recv()

        def body(rows):
            s_hl[i, rows, :] = beside(s_in[i, rows, :])

        tiles(leaf, LANES, body)

    for g, swap in zip(near_gs, near_swaps):
        swap.wait_recv()
        g.ring1()
        g.ring2(0)
    own_partial(0)
    own_sums(0)
    for g in near_gs:
        for off1 in (3, 1, 2):
            g.ring1_recv(off1)
            g.ring2(off1)
        g.ring2_pass(0)
    for g in near_gs:
        g.to_twin(0)
    own_partial(1)
    for g in near_gs:
        for off1 in (3, 1, 2):
            g.ring2_pass(off1)
    wt_g.ring2(0)
    for off1 in (3, 1, 2):
        wt_g.ring1_recv(off1)
        wt_g.ring2(off1)
    for g in near_gs:
        g.to_twin(3)
        g.to_twin(1)
    key_swap.wait_recv()
    make_one_hot(5, key_in, place.cross[0])
    split_swapped(0)
    for off1 in (0, 3, 1, 2):
        near_gs[0].end_to_twin(off1)
    for i in range(2, last):
        own_partial(i)
    for off1 in (0, 3, 1, 2):
        near_gs[1].end_to_twin(off1)
    wt_g.to_twin(0)

    def split_partner(h):
        count = 4 * nqp[h].shape[1]

        def body(index, carry):
            rows = pl.ds(pl.multiple_of(h * cut + index * count, count), count)
            block = nqp[h][pl.ds(4 * index, 4)].reshape(count, leaf)
            nq_hi[rows, :], nq_lo[rows, :] = halves(block)
            return carry

        lax.fori_loop(0, group // 4, body, 0)

    z_swaps, t_swaps = {}, {}

    def near_chunk(i):
        if i > 0:
            split_swapped(i)
        if i == 0:
            for h in range(2):
                near_gs[h].from_twin()
                split_partner(h)
                partial_rows(i, span[h])
                if h == 0:
                    for rows in row_parts:
                        y_out[i, rows, :] += fold(dot(oh[5, rows, span[0]], p_hl[i, span[0], :]))
        else:
            partial(i)
        sum_swaps[i] = []
        for k, rows in enumerate(row_parts):
            if i == 0:
                y_out[i, rows, :] += fold(dot(oh[5, rows, span[1]], p_hl[i, span[1], :]))
            else:
                y_out[i, rows, :] += sums(5, i, rows)
            sum_swaps[i].append(send_sums(i, k))
        if i == 0:
            make_one_hot(4, key_in, place.leaf)

        def here(rows):
            x[rows, lane(i)] += sums(4, i, rows)

        tiles(leaf, leaf_tile, here)

    def pass_on():
        far_swap.wait_recv()

        def body(rows):
            u_out[rows, :] += w_in[rows, :]

        tiles(leaf, LANES, body)
        return send(u_out, u_in, once, 4, place.mate)

    def weights():
        count = inverse.shape[0]
        scale = [1.0 / math.sqrt(2**k * leaf) for k in range(2)]

        def split(pair, carry):
            rows = pl.ds(pl.multiple_of(pair * 2 * count, 16), 2 * count)
            other = RING * RING + (pair % RING) * RING + pair // RING
            both = jnp.concatenate([wt[pair], wt[other]], axis=0)
            ws_hi[rows, :], ws_lo[rows, :] = halves(both[:, : leaf + 4 * rank])
            for k in range(2):
                at = leaf + (4 + k) * rank
                v_all[rows, pl.ds(k * rank, rank)] = both[:, at : at + rank] * scale[k]
            return carry

        lax.fori_loop(0, RING * RING, split, 0)
        vt_hi[...], vt_lo[...] = halves(v_all[...].T)
        second_v = pl.ds(rank, rank)
        first_w = pl.ds(leaf, 2 * rank)
        m_out[...] = dot3(vt_hi[second_v, :], vt_lo[second_v, :], ws_hi[:, first_w], ws_lo[:, first_w])
        mine_m = half_m()
        swap = send(m_out.at[mine_m], m_in.at[mine_m], once, 5, place.mate)
        step = min(256, leaf)
        for k in range(leaf // step):
            block = pl.ds(k * step, step)
            r = dot3(vt_hi[...], vt_lo[...], ws_hi[:, block], ws_lo[:, block])
            b_hi[:, block], b_lo[:, block] = halves(r)
        for k in range(2):
            block, source = pl.ds(2 * k * rank, 2 * rank), pl.ds(leaf + 2 * k * rank, 2 * rank)

            def body(rows):
                wn_hi[rows, block] = dot(gt[rows, :], ws_hi[:, source]).astype(BF16)
                wn_lo[rows, block] = dot(gt[rows, :], ws_lo[:, source]).astype(BF16)

            tiles(leaf, leaf_tile, body)
        return swap

    def half_m():
        return pl.ds(pl.multiple_of(place.core * (rank // 2), rank // 2), rank // 2)

    def corrections_pass(swap):
        swap.wait_recv()
        ref = m_in.at[half_m()]
        return send(ref, ref, once, 6, place.twin)

    def corrections(swap):
        swap.wait_recv()
        one, two = pl.ds(0, rank), pl.ds(rank, rank)
        k_hi[:, one], k_lo[:, one] = halves(m_out[:, one] + m_in[:, two])
        k_hi[:, two], k_lo[:, two] = halves(m_out[:, two] + m_in[:, one])

    one, two = pl.ds(0, rank), pl.ds(rank, rank)
    state_columns = pl.ds(0, leaf)

    def correct(rows, i, at, size):
        block = pl.ds(at * rank, size * rank)
        nat[rows, lane(i)] -= dot_beside(wn_hi[rows, block], wn_lo[rows, block], c_hl[block, :])

    def first(i, more=None):
        if more is not None:
            more.wait_recv()
        z = None
        for k, rows in enumerate(row_parts):
            sum_swaps[i][k].wait_recv()
            whole = x[rows, lane(i)] + y_in[i, rows, :]
            x_hl[rows, :] = beside(whole if more is None else whole + u_in[rows, :])
            term = dot_beside(b_hi[:, rows], b_lo[:, rows], x_hl[rows, :])
            z = term if z is None else z + term
        z_out[i] = z
        if i == direct:
            own_swaps.append(send(z_out.at[i, one], z_in.at[i, one], once, 8, place.mate))
            own = beside(z_out[i, one, :])
            z_out[i, two, :] = z_out[i, two, :] - dot_beside(k_hi[:, two], k_lo[:, two], own)
            own_swaps.append(send(z_out.at[i, two], far_in, once, 7, place.far))
            own_swaps.append(send(z_out.at[i, two], t_in.at[i], per, (3, i), place.cross))
            own_swaps.append(send(z_out.at[i, two], z_in.at[i, two], per, (2, i), place.mate))
        else:
            z_swaps[i] = send(z_out.at[i], z_in.at[i], per, (2, i), place.mate)

        def state(rows):
            st_hl[rows, :] = beside(dot_beside(ws_hi[rows, state_columns], ws_lo[rows, state_columns], x_hl[...]))

        tiles(leaf, leaf_tile, state)

        def natural(rows):
            nat[rows, lane(i)] = fold(dot(gt[rows, :], st_hl[...]))

        tiles(leaf, leaf_tile, natural)

    def second(i):
        z_swaps[i].wait_recv()
        c_hl[one, :] = beside(z_in[i, one, :])
        c_hl[two, :] = beside(z_out[i, one, :])
        both = pl.ds(0, 2 * rank)
        total = z_out[i, two, :] + z_in[i, two, :] - dot_beside(k_hi[...], k_lo[...], c_hl[both, :])
        t_out[i] = total
        t_swaps[i] = send(t_out.at[i], t_in.at[i], per, (3, i), place.cross)
        c_hl[pl.ds(3 * rank, rank), :] = beside(total)

        def update(rows):
            correct(rows, i, 0, 2)
            correct(rows, i, 3, 1)

        tiles(leaf, leaf_tile, update)

    def third(i):
        t_swaps[i].wait_recv()
        c_hl[pl.ds(2 * rank, rank), :] = beside(t_in[i])
        tiles(leaf, leaf_tile, lambda rows: correct(rows, i, 2, 1))

    def at_once(i):
        for copy in own_swaps:
            copy.wait_recv()
        c_hl[one, :] = beside(z_in[i, one, :])
        c_hl[two, :] = beside(z_out[i, one, :])
        c_hl[pl.ds(2 * rank, rank), :] = beside(t_in[i] + far_in[...])
        c_hl[pl.ds(3 * rank, rank), :] = beside(z_out[i, two, :] + z_in[i, two, :])
        tiles(leaf, leaf_tile, lambda rows: correct(rows, i, 0, 4))

    direct = last - 1
    own_swaps = []
    near_chunk(0)
    own_sums(1)
    wt_g.ring2_pass(0)
    wt_g.ring2_pass(3)
    near_chunk(1)
    wt_g.ring2_pass(1)
    wt_g.ring2_pass(2)
    own_sums(last)
    mate_sums = pass_on()
    wt_g.to_twin(3)
    wt_g.to_twin(1)
    for i in range(2, last):
        own_sums(i)
        near_chunk(i)
    for off1 in (0, 3, 1, 2):
        wt_g.end_to_twin(off1)
    wt_g.from_twin()
    m_swap = weights()
    first(0)
    first(last, mate_sums)
    m_swap = corrections_pass(m_swap)
    first(1)
    corrections(m_swap)
    for i in (0, last, 1):
        second(i)
    first(direct)
    for i in (0, last, 1):
        third(i)
    for copy in started:
        if not any(copy is other for other in own_swaps):
            copy.wait_send()
    for g in (*near_gs, wt_g):
        g.finish()
    at_once(direct)
    for copy in own_swaps:
        copy.wait_send()


def per_device(
    incident, sources, tree_order, near_quad, near_owner, near_slot, leaf_inverse, basis_v, basis_w
):
    leaf, cols = incident.shape
    near = near_quad.shape[0]
    rank = basis_v.shape[2]
    group = lax.axis_size("col")
    rows = leaf // group
    chunks = cols // LANES
    width = leaf + 6 * rank
    vmem, sem = pltpu.VMEM, pltpu.SemaphoreType.DMA

    def f32(*shape):
        return vmem(shape, F32)

    def pair(*shape):
        return [vmem(shape, BF16), vmem(shape, BF16)]

    scratch = [
        vmem((1, leaf), jnp.int32), vmem((1, near), jnp.int32), vmem((1, near), jnp.int32),
        f32(rows, leaf), f32(2, rows, rank), f32(2, 2, rows, rank),
        f32(near, leaf), f32(leaf, cols), f32(leaf, cols),
        f32(group, 3 * near // (4 * group), leaf), f32(group, near // (4 * group), leaf), f32(group, rows, width),
        vmem((1, near), jnp.int32), vmem((1, near), jnp.int32),
        f32(chunks, leaf, LANES), f32(chunks, leaf, LANES), f32(chunks, leaf, LANES),
        f32(chunks, 2 * rank, LANES), f32(chunks, 2 * rank, LANES),
        f32(chunks, rank, LANES), f32(chunks, rank, LANES),
        f32(leaf, LANES), f32(leaf, LANES), f32(leaf, LANES), f32(leaf, LANES),
        f32(rank, 2 * rank), f32(rank, 2 * rank), f32(rank, LANES),
        *pair(near, leaf), vmem((chunks, leaf, 2 * LANES), BF16), vmem((chunks, near, 2 * LANES), BF16),
        vmem((6, leaf, near), BF16), vmem((leaf, leaf), BF16),
        *pair(2 * rank, leaf), *pair(2 * rank, leaf),
        *pair(leaf, leaf + 4 * rank), *pair(leaf, 4 * rank),
        *pair(rank, 2 * rank), vmem((leaf, 2 * LANES), BF16), vmem((4 * rank, 2 * LANES), BF16),
        vmem((leaf, 2 * LANES), BF16), f32(leaf, 2 * rank),
        sem((3, 32)), sem((3, 32)), sem((5, chunks)), sem((5, chunks)), sem((9,)), sem((9,)),
        sem((10,)),
    ]
    in_any = pl.BlockSpec(memory_space=pl.ANY)
    return pl.pallas_call(
        kernel,
        out_shape=pltpu.VMEM((leaf, cols), F32),
        in_specs=[in_any] * 9,
        out_specs=pl.BlockSpec(memory_space=pltpu.VMEM),
        scratch_shapes=scratch,
        compiler_params=pltpu.CompilerParams(
            collective_id=0, has_side_effects=True, vmem_limit_bytes=54 * 1024 * 1024
        ),
        cost_estimate=pl.CostEstimate(flops=15 * 10**9, bytes_accessed=12 * 10**6, transcendentals=0),
    )(
        tree_order, near_owner.reshape(1, near), near_slot.reshape(1, near),
        leaf_inverse, basis_v, basis_w, incident, sources, near_quad,
    )

def solution(mesh):
    placed = (
        P("leaf", "col"),
        P("leaf", "col"),
        P("leaf", None),
        P("leaf", None),
        P("leaf", None),
        P("leaf"),
        P(("leaf", "col"), None),
        P(None, ("leaf", "col"), None),
        P(None, None, ("leaf", "col"), None),
    )
    return jax.shard_map(
        per_device, mesh=mesh, in_specs=placed, out_specs=P("leaf", "col"), check_vma=False
    )
```

```python
import functools
import math

import jax
import jax.numpy as jnp
from jax import lax
from jax.experimental import pallas as pl
from jax.experimental.pallas import tpu as pltpu
from jax.sharding import PartitionSpec as P

MESH = pl.DeviceIdType.MESH
F32 = jnp.float32
BF16 = jnp.bfloat16
LANES = 128
RING = 4


def halves(value):
    top = value.astype(BF16)
    return top, (value - top.astype(F32)).astype(BF16)


def dot(a, b):
    return jnp.dot(a, b, preferred_element_type=F32)


def dot3(a_hi, a_lo, b_hi, b_lo):
    return dot(a_hi, b_hi) + dot(a_hi, b_lo) + dot(a_lo, b_hi)


def beside(value):
    return jnp.concatenate(halves(value), axis=1)


def fold(wide):
    return wide[:, :LANES] + wide[:, LANES:]


def dot_beside(a_hi, a_lo, b):
    return fold(dot(a_hi, b)) + dot(a_lo, b[:, :LANES])


def tiles(count, size, body):
    def step(index, carry):
        body(pl.ds(pl.multiple_of(index * size, size), size))
        return carry

    lax.fori_loop(0, count // size, step, 0)


class Place:
    def __init__(self):
        self.leaf = lax.axis_index("leaf")
        self.col = lax.axis_index("col")
        self.core = self.col % 2
        y = (self.col // 2) % RING
        z = self.col // (2 * RING)
        self.d1 = y * (1 - self.core) + z * self.core
        self.d2 = z * (1 - self.core) + y * self.core
        self.twin = (self.leaf, self.col + 1 - 2 * self.core)
        self.mate = (self.leaf + 1 - 2 * (self.leaf % 2), self.col)
        self.cross = (3 - self.leaf, self.col)
        self.right1 = self.device(0, 1)
        self.left1 = self.device(0, RING - 1)
        self.opposite1 = self.device(0, 2)
        self.far = (self.leaf + 2 - 4 * (self.leaf // 2), self.col)
        self.right2 = self.device(1, 0)
        self.left2 = self.device(RING - 1, 0)

    def device(self, off2, off1):
        a, b, core = (self.d2 + off2) % RING, (self.d1 + off1) % RING, self.core
        return self.leaf, (a * 2 * RING + b * 2) * (1 - core) + (b * 2 * RING + a * 2 + 1) * core

    def group(self, off2):
        return (self.core * RING + (self.d2 + off2) % RING) * RING

    def twin_group(self, off2):
        return ((1 - self.core) * RING + (self.d1 + off2) % RING) * RING

    def index(self, off2, off1):
        return self.group(off2) + (self.d1 + off1) % RING

    def twin_index(self, off2, off1):
        return self.twin_group(off2) + (self.d2 + off1) % RING


class Gather:
    def __init__(self, place, buf, send_sem, recv_sem):
        self.p, self.buf, self.ss, self.rs = place, buf, send_sem, recv_sem
        self.started = []

    def piece(self, off2, off1):
        return self.buf.at[self.p.index(off2, off1)]

    def send(self, ref, sem, device):
        copy = pltpu.make_async_remote_copy(
            src_ref=ref, dst_ref=ref, send_sem=self.ss.at[sem], recv_sem=self.rs.at[sem],
            device_id=device, device_id_type=MESH,
        )
        copy.start()
        self.started.append(copy)

    def recv(self, ref, sem):
        pltpu.make_async_remote_copy(
            src_ref=ref, dst_ref=ref, send_sem=self.ss.at[sem], recv_sem=self.rs.at[sem],
            device_id=self.p.twin, device_id_type=MESH,
        ).wait_recv()

    def ring1(self):
        own = self.piece(0, 0)
        self.send(own, 0, self.p.right1)
        self.send(own, 1, self.p.left1)
        self.send(own, 2, self.p.opposite1)

    def ring1_recv(self, off1):
        self.recv(self.piece(0, off1), (3, 1, 2).index(off1))

    def ring2(self, off1):
        self.send(self.piece(0, off1), 4 + off1, self.p.right2)
        self.send(self.piece(0, off1), 8 + off1, self.p.left2)

    def ring2_pass(self, off1):
        self.recv(self.piece(3, off1), 4 + off1)
        if off1 in (0, 1):
            self.send(self.piece(3, off1), 12 + off1, self.p.right2)
        self.recv(self.piece(1, off1), 8 + off1)
        if off1 in (3, 2):
            self.send(self.piece(1, off1), 12 + off1, self.p.left2)

    def ring2_end(self, off1):
        self.recv(self.piece(2, off1), 12 + off1)

    def to_twin(self, off2):
        self.send(self.buf.at[pl.ds(self.p.group(off2), RING)], 16 + off2, self.p.twin)

    def end_to_twin(self, off1):
        self.ring2_end(off1)
        self.send(self.piece(2, off1), 20 + off1, self.p.twin)

    def from_twin(self):
        for off2 in (0, 3, 1):
            self.recv(self.buf.at[pl.ds(self.p.twin_group(off2), RING)], 16 + off2)
        for off1 in (0, 3, 1, 2):
            self.recv(self.buf.at[self.p.twin_index(2, off1)], 20 + off1)

    def finish(self):
        for copy in self.started:
            copy.wait_send()


def kernel(
    tree_any, owner_any, slot_any, inverse_any, basis_v_any, basis_w_any, incident, sources, near_quad, nat,
    tree, owner, slot, inverse, basis_v, basis_w,
    nq, s_own, x, nqp, wt, key_out, key_in, s_in, y_out, y_in, z_out, z_in, t_out, t_in, u_out, u_in, w_out, w_in,
    m_out, m_in, far_in,
    nq_hi, nq_lo, s_hl, p_hl, oh, gt, vt_hi, vt_lo, b_hi, b_lo, ws_hi, ws_lo, wn_hi, wn_lo,
    k_hi, k_lo, x_hl, c_hl, st_hl, v_all,
    gsend, grecv, csend, crecv, osend, orecv, load_sem,
):
    leaf, cols = incident.shape
    near = near_quad.shape[0]
    rank = basis_v.shape[2]
    part = nqp.shape[2]
    group = nqp.shape[1]
    chunks = cols // LANES
    last = chunks - 1
    near_tile, leaf_tile = near // 2, leaf // 2
    row_parts = (pl.ds(0, 2 * leaf // 3), pl.ds(2 * leaf // 3, leaf // 3))
    place = Place()
    mine = place.index(0, 0)
    started = []

    def lane(i):
        return pl.ds(i * LANES, LANES)

    others = pl.ds(0, last * LANES)
    pairs = (
        (tree_any, tree), (owner_any, owner), (slot_any, slot), (inverse_any, inverse), (basis_v_any, basis_v),
        (basis_w_any, basis_w), (near_quad, nq), (sources.at[:, lane(last)], s_own.at[:, lane(last)]), (incident, x),
        (sources.at[:, others], s_own.at[:, others]),
    )
    loads = [pltpu.make_async_copy(src, dst, load_sem.at[i]) for i, (src, dst) in enumerate(pairs)]
    barrier = pltpu.get_barrier_semaphore()
    neighbours = (
        place.mate, place.cross, place.far, place.twin, place.right1, place.left1, place.opposite1, place.right2,
        place.left2,
    )
    for device in neighbours:
        pl.semaphore_signal(barrier, inc=1, device_id=device, device_id_type=MESH)
    for copy in loads[:8]:
        copy.start()

    def send(src, dst, sems, index, device):
        copy = pltpu.make_async_remote_copy(
            src_ref=src, dst_ref=dst, send_sem=sems[0].at[index], recv_sem=sems[1].at[index],
            device_id=device, device_id_type=MESH,
        )
        copy.start()
        started.append(copy)
        return copy

    near_gs = [Gather(place, nqp.at[h], gsend.at[h], grecv.at[h]) for h in range(2)]
    wt_g = Gather(place, wt, gsend.at[2], grecv.at[2])

    def make_gt(rows):
        number = rows.start + lax.broadcasted_iota(jnp.int32, (rows.size, leaf), 0)
        gt[rows, :] = jnp.where(number == tree[...], 1.0, 0.0).astype(BF16)

    def make_one_hot(which, key, block):
        base = block * leaf

        def body(rows):
            number = base + rows.start + lax.broadcasted_iota(jnp.int32, (rows.size, near), 0)
            oh[which, rows, :] = jnp.where(number == key[0:1, :], 1.0, 0.0).astype(BF16)

        tiles(leaf, LANES, body)

    def split_near(rows):
        nq_hi[rows, :], nq_lo[rows, :] = halves(nq[rows, :])

    def partial_rows(i, rows):
        p_hl[i, rows, :] = beside(dot_beside(nq_hi[rows, :], nq_lo[rows, :], s_hl[i]))

    def partial(i):
        tiles(near, near_tile, lambda rows: partial_rows(i, rows))

    def own_partial(i):
        def body(rows):
            s_hl[i, rows, :] = beside(s_own[rows, lane(i)])

        tiles(leaf, LANES, body)
        partial(i)

    def sums(which, i, rows):
        return fold(dot(oh[which, rows, :], p_hl[i]))

    for copy in loads[:6]:
        copy.wait()
    key_out[...] = owner[...] * leaf + slot[...]
    tiles(leaf, LANES, make_gt)
    nt = (((1,), (1,)), ((), ()))
    top, low = halves(inverse[...])
    wt[mine, :, pl.ds(0, leaf)] = lax.dot_general(
        top, gt[...], nt, preferred_element_type=F32
    ) + lax.dot_general(low, gt[...], nt, preferred_element_type=F32)
    for k in range(4):
        wt[mine, :, pl.ds(leaf + k * rank, rank)] = basis_w[k // 2, k % 2]
    for k in range(2):
        wt[mine, :, pl.ds(leaf + (4 + k) * rank, rank)] = basis_v[k]

    pl.semaphore_wait(barrier, len(neighbours))

    once, per = (osend, orecv), (csend, crecv)
    near_swaps = [
        send(
            near_quad.at[pl.ds(pl.multiple_of(h * near // 2 + mine * part, part), part)], nqp.at[h, mine],
            once, h, place.mate,
        )
        for h in range(2)
    ]
    key_swap = send(key_out, key_in, once, 2, place.mate)
    wt_g.ring1()
    source_swaps = [
        send(sources.at[:, lane(i)], s_in.at[i], per, (0, i), place.mate) for i in range(last)
    ]

    def send_sums(i, part):
        rows = row_parts[part]
        return send(y_out.at[i, rows], y_in.at[i, rows], per, (1 + 3 * part, i), place.cross)

    for copy in loads[8:]:
        copy.start()
    loads[6].wait()
    tiles(near, LANES, split_near)
    loads[7].wait()
    own_partial(last)
    make_one_hot(1, key_out, place.cross[0])
    sum_swaps = {last: []}
    for k in range(2):
        y_out[last, row_parts[k], :] = sums(1, last, row_parts[k])
        sum_swaps[last].append(send_sums(last, k))

    make_one_hot(3, key_out, place.far[0])

    def last_far(rows):
        w_out[rows, :] = sums(3, last, rows)

    tiles(leaf, leaf_tile, last_far)
    far_swap = send(w_out, w_in, once, 3, place.cross)
    make_one_hot(0, key_out, place.leaf)
    make_one_hot(2, key_out, place.mate[0])
    loads[8].wait()
    loads[9].wait()

    def own_sums(i):
        def body(rows):
            x[rows, lane(i)] += sums(0, i, rows)
            if i < last:
                y_out[i, rows, :] = sums(1, i, rows)
            else:
                u_out[rows, :] = sums(2, i, rows)

        tiles(leaf, leaf_tile, body)

    def split_swapped(i):
        source_swaps[i].wait_recv()

        def body(rows):
            s_hl[i, rows, :] = beside(s_in[i, rows, :])

        tiles(leaf, LANES, body)

    for g, swap in zip(near_gs, near_swaps):
        swap.wait_recv()
        g.ring1()
        g.ring2(0)
    own_partial(0)
    own_sums(0)
    for g in near_gs:
        for off1 in (3, 1, 2):
            g.ring1_recv(off1)
            g.ring2(off1)
        g.ring2_pass(0)
    for g in near_gs:
        g.to_twin(0)
    own_partial(1)
    for g in near_gs:
        for off1 in (3, 1, 2):
            g.ring2_pass(off1)
    wt_g.ring2(0)
    for off1 in (3, 1, 2):
        wt_g.ring1_recv(off1)
        wt_g.ring2(off1)
    for g in near_gs:
        g.to_twin(3)
        g.to_twin(1)
    key_swap.wait_recv()
    make_one_hot(5, key_in, place.cross[0])
    split_swapped(0)
    for off1 in (0, 3, 1, 2):
        near_gs[0].end_to_twin(off1)
    for i in range(2, last):
        own_partial(i)
    for off1 in (0, 3, 1, 2):
        near_gs[1].end_to_twin(off1)
    wt_g.to_twin(0)

    def split_partner(h):
        count = 4 * part

        def body(index, carry):
            rows = pl.ds(pl.multiple_of(h * near // 2 + index * count, count), count)
            block = nqp[h, pl.ds(4 * index, 4)].reshape(count, leaf)
            nq_hi[rows, :], nq_lo[rows, :] = halves(block)
            return carry

        lax.fori_loop(0, group // 4, body, 0)

    z_swaps, t_swaps = {}, {}

    def near_chunk(i):
        if i > 0:
            split_swapped(i)
        if i == 0:
            span = [pl.ds(h * near // 2, near // 2) for h in range(2)]
            for h in range(2):
                near_gs[h].from_twin()
                split_partner(h)
                partial_rows(i, span[h])
                if h == 0:
                    for rows in row_parts:
                        y_out[i, rows, :] += fold(dot(oh[5, rows, span[0]], p_hl[i, span[0], :]))
        else:
            partial(i)
        sum_swaps[i] = []
        for k, rows in enumerate(row_parts):
            if i == 0:
                y_out[i, rows, :] += fold(dot(oh[5, rows, span[1]], p_hl[i, span[1], :]))
            else:
                y_out[i, rows, :] += sums(5, i, rows)
            sum_swaps[i].append(send_sums(i, k))
        if i == 0:
            make_one_hot(4, key_in, place.leaf)

        def here(rows):
            x[rows, lane(i)] += sums(4, i, rows)

        tiles(leaf, leaf_tile, here)

    def pass_on():
        far_swap.wait_recv()

        def body(rows):
            u_out[rows, :] += w_in[rows, :]

        tiles(leaf, LANES, body)
        return send(u_out, u_in, once, 4, place.mate)

    def weights():
        count = inverse.shape[0]
        scale = [1.0 / math.sqrt(2**k * leaf) for k in range(2)]

        def split(pair, carry):
            rows = pl.ds(pl.multiple_of(pair * 2 * count, 16), 2 * count)
            other = RING * RING + (pair % RING) * RING + pair // RING
            both = jnp.concatenate([wt[pair], wt[other]], axis=0)
            ws_hi[rows, :], ws_lo[rows, :] = halves(both[:, : leaf + 4 * rank])
            for k in range(2):
                at = leaf + (4 + k) * rank
                v_all[rows, pl.ds(k * rank, rank)] = both[:, at : at + rank] * scale[k]
            return carry

        lax.fori_loop(0, RING * RING, split, 0)
        vt_hi[...], vt_lo[...] = halves(v_all[...].T)
        second_v = pl.ds(rank, rank)
        first_w = pl.ds(leaf, 2 * rank)
        m_out[...] = dot3(vt_hi[second_v, :], vt_lo[second_v, :], ws_hi[:, first_w], ws_lo[:, first_w])
        mine_m = half_m()
        swap = send(m_out.at[mine_m], m_in.at[mine_m], once, 5, place.mate)
        step = min(256, leaf)
        for k in range(leaf // step):
            block = pl.ds(k * step, step)
            r = dot3(vt_hi[...], vt_lo[...], ws_hi[:, block], ws_lo[:, block])
            b_hi[:, block], b_lo[:, block] = halves(r)
        for k in range(2):
            block, source = pl.ds(2 * k * rank, 2 * rank), pl.ds(leaf + 2 * k * rank, 2 * rank)

            def body(rows):
                wn_hi[rows, block] = dot(gt[rows, :], ws_hi[:, source]).astype(BF16)
                wn_lo[rows, block] = dot(gt[rows, :], ws_lo[:, source]).astype(BF16)

            tiles(leaf, leaf_tile, body)
        return swap

    def half_m():
        return pl.ds(pl.multiple_of(place.core * (rank // 2), rank // 2), rank // 2)

    def corrections_pass(swap):
        swap.wait_recv()
        ref = m_in.at[half_m()]
        return send(ref, ref, once, 6, place.twin)

    def corrections(swap):
        swap.wait_recv()
        one, two = pl.ds(0, rank), pl.ds(rank, rank)
        k_hi[:, one], k_lo[:, one] = halves(m_out[:, one] + m_in[:, two])
        k_hi[:, two], k_lo[:, two] = halves(m_out[:, two] + m_in[:, one])

    one, two = pl.ds(0, rank), pl.ds(rank, rank)
    state_columns = pl.ds(0, leaf)

    def correct(rows, i, at, size):
        block = pl.ds(at * rank, size * rank)
        nat[rows, lane(i)] -= dot_beside(wn_hi[rows, block], wn_lo[rows, block], c_hl[block, :])

    def first(i, more=None):
        if more is not None:
            more.wait_recv()
        z = None
        for k, rows in enumerate(row_parts):
            sum_swaps[i][k].wait_recv()
            whole = x[rows, lane(i)] + y_in[i, rows, :]
            x_hl[rows, :] = beside(whole if more is None else whole + u_in[rows, :])
            term = dot_beside(b_hi[:, rows], b_lo[:, rows], x_hl[rows, :])
            z = term if z is None else z + term
        z_out[i] = z
        if i == direct:
            own_swaps.append(send(z_out.at[i, one], z_in.at[i, one], once, 8, place.mate))
            own = beside(z_out[i, one, :])
            z_out[i, two, :] = z_out[i, two, :] - dot_beside(k_hi[:, two], k_lo[:, two], own)
            own_swaps.append(send(z_out.at[i, two], far_in, once, 7, place.far))
            own_swaps.append(send(z_out.at[i, two], t_in.at[i], per, (3, i), place.cross))
            own_swaps.append(send(z_out.at[i, two], z_in.at[i, two], per, (2, i), place.mate))
        else:
            z_swaps[i] = send(z_out.at[i], z_in.at[i], per, (2, i), place.mate)

        def state(rows):
            st_hl[rows, :] = beside(dot_beside(ws_hi[rows, state_columns], ws_lo[rows, state_columns], x_hl[...]))

        tiles(leaf, leaf_tile, state)

        def natural(rows):
            nat[rows, lane(i)] = fold(dot(gt[rows, :], st_hl[...]))

        tiles(leaf, leaf_tile, natural)

    def second(i):
        z_swaps[i].wait_recv()
        c_hl[one, :] = beside(z_in[i, one, :])
        c_hl[two, :] = beside(z_out[i, one, :])
        both = pl.ds(0, 2 * rank)
        total = z_out[i, two, :] + z_in[i, two, :] - dot_beside(k_hi[...], k_lo[...], c_hl[both, :])
        t_out[i] = total
        t_swaps[i] = send(t_out.at[i], t_in.at[i], per, (3, i), place.cross)
        c_hl[pl.ds(3 * rank, rank), :] = beside(total)

        def update(rows):
            correct(rows, i, 0, 2)
            correct(rows, i, 3, 1)

        tiles(leaf, leaf_tile, update)

    def third(i):
        t_swaps[i].wait_recv()
        c_hl[pl.ds(2 * rank, rank), :] = beside(t_in[i])
        tiles(leaf, leaf_tile, lambda rows: correct(rows, i, 2, 1))

    def at_once(i):
        for copy in own_swaps:
            copy.wait_recv()
        c_hl[one, :] = beside(z_in[i, one, :])
        c_hl[two, :] = beside(z_out[i, one, :])
        c_hl[pl.ds(2 * rank, rank), :] = beside(t_in[i] + far_in[...])
        c_hl[pl.ds(3 * rank, rank), :] = beside(z_out[i, two, :] + z_in[i, two, :])
        tiles(leaf, leaf_tile, lambda rows: correct(rows, i, 0, 4))

    direct = last - 1
    own_swaps = []
    near_chunk(0)
    own_sums(1)
    wt_g.ring2_pass(0)
    wt_g.ring2_pass(3)
    near_chunk(1)
    wt_g.ring2_pass(1)
    wt_g.ring2_pass(2)
    own_sums(last)
    mate_sums = pass_on()
    wt_g.to_twin(3)
    wt_g.to_twin(1)
    for i in range(2, last):
        own_sums(i)
        near_chunk(i)
    for off1 in (0, 3, 1, 2):
        wt_g.end_to_twin(off1)
    wt_g.from_twin()
    m_swap = weights()
    first(0)
    first(last, mate_sums)
    m_swap = corrections_pass(m_swap)
    first(1)
    corrections(m_swap)
    for i in (0, last, 1):
        second(i)
    first(direct)
    for i in (0, last, 1):
        third(i)
    for copy in started:
        if not any(copy is other for other in own_swaps):
            copy.wait_send()
    for g in (*near_gs, wt_g):
        g.finish()
    at_once(direct)
    for copy in own_swaps:
        copy.wait_send()


def per_device(
    incident, sources, tree_order, near_quad, near_owner, near_slot, leaf_inverse, basis_v, basis_w
):
    leaf, cols = incident.shape
    near = near_quad.shape[0]
    rank = basis_v.shape[2]
    group = lax.axis_size("col")
    rows = leaf // group
    chunks = cols // LANES
    width = leaf + 6 * rank
    vmem, sem = pltpu.VMEM, pltpu.SemaphoreType.DMA

    def f32(*shape):
        return vmem(shape, F32)

    def pair(*shape):
        return [vmem(shape, BF16), vmem(shape, BF16)]

    scratch = [
        vmem((1, leaf), jnp.int32), vmem((1, near), jnp.int32), vmem((1, near), jnp.int32),
        f32(rows, leaf), f32(2, rows, rank), f32(2, 2, rows, rank),
        f32(near, leaf), f32(leaf, cols), f32(leaf, cols),
        f32(2, group, near // (2 * group), leaf), f32(group, rows, width),
        vmem((1, near), jnp.int32), vmem((1, near), jnp.int32),
        f32(chunks, leaf, LANES), f32(chunks, leaf, LANES), f32(chunks, leaf, LANES),
        f32(chunks, 2 * rank, LANES), f32(chunks, 2 * rank, LANES),
        f32(chunks, rank, LANES), f32(chunks, rank, LANES),
        f32(leaf, LANES), f32(leaf, LANES), f32(leaf, LANES), f32(leaf, LANES),
        f32(rank, 2 * rank), f32(rank, 2 * rank), f32(rank, LANES),
        *pair(near, leaf), vmem((chunks, leaf, 2 * LANES), BF16), vmem((chunks, near, 2 * LANES), BF16),
        vmem((6, leaf, near), BF16), vmem((leaf, leaf), BF16),
        *pair(2 * rank, leaf), *pair(2 * rank, leaf),
        *pair(leaf, leaf + 4 * rank), *pair(leaf, 4 * rank),
        *pair(rank, 2 * rank), vmem((leaf, 2 * LANES), BF16), vmem((4 * rank, 2 * LANES), BF16),
        vmem((leaf, 2 * LANES), BF16), f32(leaf, 2 * rank),
        sem((3, 32)), sem((3, 32)), sem((5, chunks)), sem((5, chunks)), sem((9,)), sem((9,)),
        sem((10,)),
    ]
    in_any = pl.BlockSpec(memory_space=pl.ANY)
    return pl.pallas_call(
        kernel,
        out_shape=pltpu.VMEM((leaf, cols), F32),
        in_specs=[in_any] * 9,
        out_specs=pl.BlockSpec(memory_space=pltpu.VMEM),
        scratch_shapes=scratch,
        compiler_params=pltpu.CompilerParams(
            collective_id=0, has_side_effects=True, vmem_limit_bytes=54 * 1024 * 1024
        ),
        cost_estimate=pl.CostEstimate(flops=15 * 10**9, bytes_accessed=12 * 10**6, transcendentals=0),
    )(
        tree_order, near_owner.reshape(1, near), near_slot.reshape(1, near),
        leaf_inverse, basis_v, basis_w, incident, sources, near_quad,
    )

def solution(mesh):
    placed = (
        P("leaf", "col"),
        P("leaf", "col"),
        P("leaf", None),
        P("leaf", None),
        P("leaf", None),
        P("leaf"),
        P(("leaf", "col"), None),
        P(None, ("leaf", "col"), None),
        P(None, None, ("leaf", "col"), None),
    )
    return jax.shard_map(
        per_device, mesh=mesh, in_specs=placed, out_specs=P("leaf", "col"), check_vma=False
    )
```
